512 devices in a mesh: rows: 64 (over y, z), rep: 8 (over x, core).
Axes of the slice: x: 4, y: 4, z: 16, core: 2. Of those that a mesh axis runs over, the one named last changes fastest.
Arguments:
- features: bfloat16 [65536, 512], P('rows', 'rep'), may hold values from -6 to 6
- neighbor_blocks: int32 [512, 2], P('rows'), may hold values from 0 to 511, as said below
- adjacency: bfloat16 [512, 2, 128, 128], P('rows'), may hold values from 0 to 100, as said below
- w_self: bfloat16 [512, 512], replicated, may hold values from -0.25 to 0.25
- w_neigh: bfloat16 [512, 512], replicated, may hold values from -0.25 to 0.25
- cotangent: bfloat16 [65536, 512], P(('rows', 'rep')), may hold values from -0.09375 to 0.09375
Outputs:
- output: bfloat16 [65536, 512], P(('rows', 'rep'))
- weight_grads: float32 [2, 512, 512], P(None, 'rows', 'rep')
The draws below stay inside these ranges and needn't reach their ends.
Inputs may be any that keep to these rules, and one draw needn't show every extreme that they name: `neighbor_blocks`: column block c belongs to index c // 8 of rows. Over the 16 entries of one index of rows, no index of rows is named more than 2 times, and some index of rows is named exactly 2 times by every index of rows. `adjacency`: entries are zero or positive.
All inputs are finite; a program needn't handle non-finite values.
Results may differ from the reference program's by a relative error of at most 0.006.
Values may be sent and summed in bfloat16 or wider, within the bound.
A program may use at most 64 MiB of HBM per device.

```python
import math
import jax
import jax.numpy as jnp
from jax import lax

F = 512
BLK = 128
K = 2
RB_DEV = 8
NBLK = 512
NODES = 65536


def draw_neighbor_blocks(key, part):
    row_count = NBLK // RB_DEV
    use_count = RB_DEV * K
    capacity = max(2, (2 * use_count + row_count - 1) // row_count)
    hot_owner = jax.random.randint(jax.random.fold_in(key, 1), (), 0, row_count)
    others = jnp.tile(jnp.arange(row_count - 1, dtype=jnp.int32), capacity)

    def one_row(sub_key):
        key_pick, key_order, key_local = jax.random.split(sub_key, 3)
        picked = jax.random.permutation(key_pick, others)[:use_count - capacity]
        owner_list = jnp.concatenate([jnp.full((capacity,), -1, jnp.int32), picked])
        owner_list = (hot_owner + 1 + owner_list) % row_count
        owner_list = jax.random.permutation(key_order, owner_list)
        local_ids = jax.random.randint(key_local, (use_count,), 0, RB_DEV)
        return (owner_list * RB_DEV + local_ids).reshape(RB_DEV, K)
    row_keys = jax.random.split(jax.random.fold_in(key, 2), row_count)
    return jax.vmap(one_row)(row_keys).reshape(NBLK, K).astype(jnp.int32)


def draw_adjacency(key, part):
    key_rate, key_keep, key_row, key_col = jax.random.split(jax.random.fold_in(key, 3), 4)
    shape = (NBLK, K, BLK, BLK)
    rates = jnp.exp(jax.random.uniform(key_rate, shape, jnp.float32, math.log(0.2), 0.0))
    keep = jax.random.bernoulli(key_keep, 0.25, shape).astype(jnp.float32)
    row_factor = jnp.exp(jax.random.uniform(key_row, (NBLK, 1, BLK, 1), jnp.float32, 0.0, math.log(10.0)))
    col_factor = jnp.exp(jax.random.uniform(key_col, (NBLK, K, 1, BLK), jnp.float32, 0.0, math.log(10.0)))
    return (rates * keep * row_factor * col_factor).astype(jnp.bfloat16)


def raised(values, own_key, source, target, shards_of, factor):
    owner, partner = [(jnp.arange(values.shape[axis_at]) // (values.shape[axis_at] // shards_of)).reshape([-1 if axis == axis_at else 1 for axis in range(values.ndim)]) for axis_at in (source, target)]
    chosen = jax.random.permutation(own_key, shards_of)[partner]
    strong = (owner == chosen) | (owner == (partner + shards_of // 2) % shards_of)
    return jnp.where(strong, factor * values, values)


def steps_of(own_key, dims, pieces, smallest, high):
    gain, own = 1.0, jax.random.fold_in(own_key, 6)
    for dim, parts in pieces:
        draws = jnp.exp(jax.random.uniform(jax.random.fold_in(own, dim), (parts,), jnp.float32, smallest / len(pieces), high / len(pieces)))
        gain = gain * jnp.repeat(draws, dims[dim] // parts).reshape([-1 if axis == dim else 1 for axis in range(len(dims))])
    return gain


def normal_values(key, shape, scale, reach, cuts=(), kind=jnp.bfloat16):
    factor_of = steps_of(key, shape, cuts, -0.22, 0.18) if cuts else 1.0
    drawn = jax.random.normal(key, shape, jnp.float32) * scale * factor_of
    return jnp.minimum(jnp.maximum(drawn, -reach), reach).astype(kind)


def noise_with(own_key, extent, spread, reach, pieces, heavy, held_as=jnp.bfloat16):
    drawn = spread * jax.random.normal(own_key, extent, jnp.float32)
    if pieces:
        drawn = drawn * steps_of(own_key, extent, pieces, -0.22, 0.18)
    return jnp.clip(raised(drawn, jax.random.fold_in(own_key, 3), *heavy), -reach, reach).astype(held_as)


def setup_inputs(seed: int = 0) -> dict:
    key_of = jax.random.split(jax.random.key(seed), 7)
    features = normal_values(key_of[0], (NODES, F), 1.0, 6.0, ((0, 64), (1, 8)))
    neighbor_blocks = draw_neighbor_blocks(jax.random.fold_in(key_of[6], 71), 0)
    adjacency = draw_adjacency(jax.random.fold_in(key_of[6], 71), 0)
    w_self = normal_values(key_of[3], (F, F), F ** -0.5, 0.25)
    w_neigh = normal_values(key_of[4], (F, F), F ** -0.5, 0.25)
    cotangent = noise_with(key_of[5], (NODES, F), (NODES ** -0.5), 0.09375, ((0, 512),), (0, 1, 512, 6.0))
    return dict(features=features, neighbor_blocks=neighbor_blocks, adjacency=adjacency, w_self=w_self, w_neigh=w_neigh, cotangent=cotangent)


def silu_slope(pre_act):
    gate_value = jax.nn.sigmoid(pre_act)
    return gate_value * (1.0 + pre_act * (1.0 - gate_value))

def reference(features, neighbor_blocks, adjacency, w_self, w_neigh, cotangent):
    node_total, width = features.shape
    block_total = adjacency.shape[0]
    block_size = adjacency.shape[2]
    feature_tiles = features.reshape(block_total, block_size, width)
    totals = lax.optimization_barrier(jnp.sum(adjacency.astype(jnp.float32), axis=(1, 3)))
    row_scale = 1.0 / jnp.sqrt(1.0 + totals)

    def one_block(inputs):
        weights, columns, scale_rows = inputs
        picked = feature_tiles[columns.astype(jnp.int32)].astype(jnp.float32)
        raw_sum = jnp.einsum('kij,kjf->if', weights.astype(jnp.float32), picked)
        return (scale_rows[:, None] * raw_sum).astype(jnp.bfloat16)
    agg = lax.map(one_block, (adjacency, neighbor_blocks, row_scale)).reshape(node_total, width)
    pre_act = jnp.dot(features, w_self, preferred_element_type=jnp.float32) + jnp.dot(agg, w_neigh, preferred_element_type=jnp.float32)
    output = jax.nn.silu(pre_act).astype(jnp.bfloat16)
    grad_pre = (cotangent.astype(jnp.float32) * silu_slope(pre_act)).astype(jnp.bfloat16)
    grad_self = jnp.dot(features.T, grad_pre, preferred_element_type=jnp.float32)
    grad_neigh = jnp.dot(agg.T, grad_pre, preferred_element_type=jnp.float32)
    return (output, jnp.stack([grad_self, grad_neigh]))
```

```python
import jax
import jax.numpy as jnp
from jax import lax
from jax.experimental import pallas as pl
from jax.experimental.pallas import tpu as pltpu
from jax.sharding import PartitionSpec as P

Y, Z, X = 4, 16, 4
REP = 2 * X
SUB = 4
PIECE = 8 // SUB
HALF = Z // 2
MESH = pl.DeviceIdType.MESH
BF, F32 = jnp.bfloat16, jnp.float32


def dot(a, b, ca, cb):
    return lax.dot_general(a, b, (((ca,), (cb,)), ((), ())), preferred_element_type=F32)


def kernel(
    nb_ref, f_hbm, adj_hbm, ws_hbm, wn_hbm, cot_hbm,
    out_ref, wg_ref,
    zbuf, far_out, far_in, near_out, near_in, own_f, own_a, lhs, adj, ws, wn, cot,
    scale, pre_self, g_own, g_all, parts, y_in, y_sum, z_in, nb_all, nb_s,
    load_sem, zs, zr, fs, fr, as_, ar, gs, gr, ps, pr, ns, nr, ys, yr, ts, tr, us, ur,
):
    row, rep = lax.axis_index("rows"), lax.axis_index("rep")
    y, z = row // Z, lax.rem(row, Z)
    x, core = rep // 2, lax.rem(rep, 2)

    def in_rows(yy, zz):
        return {"rows": yy * Z + zz, "rep": rep}

    def in_rep(q):
        return {"rows": row, "rep": q}

    def remote(src, dst, send, recv, device):
        return pltpu.make_async_remote_copy(
            src_ref=src, dst_ref=dst, send_sem=send, recv_sem=recv,
            device_id=device, device_id_type=MESH,
        )

    def turn(a, k, n):
        return lax.rem(a + k + n, n)

    right, left = in_rows(y, turn(z, 1, Z)), in_rows(y, turn(z, -1, Z))
    y_next, y_prev, y_far = turn(y, 1, Y), turn(y, -1, Y), turn(y, 2, Y)

    first = [
        pltpu.make_async_copy(
            f_hbm.at[:, pl.ds(128 * l, 128)], zbuf.at[z * 8 + l], load_sem.at[l]
        )
        for l in range(8)
    ]
    mine = pl.ds(pl.multiple_of(core * 64, 64), 64)
    mine_a = pl.ds(pl.multiple_of(128 + core * 64, 64), 64)
    later = [
        pltpu.make_async_copy(f_hbm, lhs.at[mine], load_sem.at[8]),
        pltpu.make_async_copy(adj_hbm, adj, load_sem.at[9]),
        pltpu.make_async_copy(ws_hbm, ws, load_sem.at[10]),
        pltpu.make_async_copy(wn_hbm, wn, load_sem.at[11]),
        pltpu.make_async_copy(cot_hbm, cot, load_sem.at[12]),
    ]
    for c in first + later:
        c.start()

    barrier = pltpu.get_barrier_semaphore()
    for device in (right, left):
        pl.semaphore_signal(barrier, inc=1, device_id=device, device_id_type=MESH)
    for k in range(1, Y):
        pl.semaphore_signal(
            barrier, inc=1, device_id=in_rows(turn(y, k, Y), z), device_id_type=MESH
        )
    for k in range(1, REP):
        pl.semaphore_signal(
            barrier, inc=1, device_id=in_rep(turn(rep, k, REP)), device_id_type=MESH
        )
    nb_all[y] = nb_ref[...]
    for c in first:
        c.wait()
    pl.semaphore_wait(barrier, 2 + (Y - 1) + (REP - 1))

    def ring_copy(way, step, piece, chunk):
        at = pl.ds(chunk * 8 + piece * PIECE, PIECE)
        return remote(
            zbuf.at[at], zbuf.at[at], zs.at[way, step, piece], zr.at[way, step, piece],
            right if way == 0 else left,
        )

    def sent(way, step, piece):
        return ring_copy(way, step, piece, turn(z, -step if way == 0 else step, Z))

    def arriving(way, step, piece):
        return ring_copy(way, step, piece, turn(z, -1 - step if way == 0 else 1 + step, Z))

    def last_way(piece):
        return 0 if piece < SUB // 2 else 1

    for piece in range(SUB):
        for way in range(2):
            sent(way, 0, piece).start()

    def feature_copy(k, q, source):
        return remote(
            zbuf.at[z * 8 + q], own_f.at[pl.ds(pl.multiple_of(source * 64, 64), 64)],
            fs.at[k - 1], fr.at[k - 1], in_rep(q),
        )

    def nb_copy(k, source):
        return remote(
            nb_all.at[source], nb_all.at[source], ns.at[k - 1], nr.at[k - 1],
            in_rows(turn(y, k, Y), z),
        )

    for k in range(1, Y):
        nb_copy(k, y).start()
    for k in range(1, REP):
        feature_copy(k, turn(rep, k, REP), rep).start()
    later[0].wait()
    pair = in_rep(x * 2 + 1 - core)
    pair_f = remote(lhs.at[mine], lhs.at[mine], ps.at[0], pr.at[0], pair)
    pair_f.start()
    own_rows = pl.ds(pl.multiple_of(rep * 64, 64), 64)
    own_f[own_rows] = zbuf[z * 8 + rep]

    def ring_step(step, carry):
        for piece in range(SUB):
            for way in range(2):
                arriving(way, step - 1, piece).wait_recv()
                sent(way, step, piece).start()
        return carry

    lax.fori_loop(1, 4, ring_step, 0)

    for k in range(1, Y):
        nb_copy(k, turn(y, -k, Y)).wait_recv()
    to_smem = pltpu.make_async_copy(nb_all, nb_s, load_sem.at[13])
    to_smem.start()
    later[1].wait()
    ones = jnp.ones((8, 128), BF)
    for b in range(8):
        total = dot(ones, adj[b, 0], 1, 1) + dot(ones, adj[b, 1], 1, 1)
        scale[b] = 1.0 / jnp.sqrt(1.0 + total)
    to_smem.wait()

    lax.fori_loop(4, 6, ring_step, 0)
    for k in range(1, REP):
        feature_copy(k, rep, turn(rep, -k, REP)).wait_recv()
    later[2].wait()
    pre_self[...] = dot(own_f[...], ws[...], 0, 0)
    lax.fori_loop(6, HALF - 1, ring_step, 0)
    for piece in range(SUB):
        for way in range(2):
            arriving(way, HALF - 2, piece).wait_recv()
            if way == last_way(piece):
                sent(way, HALF - 1, piece).start()
    for piece in range(SUB):
        arriving(last_way(piece), HALF - 1, piece).wait_recv()

    def wanted(yy, u):
        return nb_s[yy, u // 8, u % 8]

    def far_copy(way):
        return remote(
            far_out.at[way], far_in.at[way], fs.at[7 + way], fr.at[7 + way],
            in_rows(y_next if way == 0 else y_prev, z),
        )

    def near_copy(way, k):
        at = pl.ds(8 * k, 8)
        return remote(
            near_out.at[way, at], near_in.at[way, at], ys.at[way, k], yr.at[way, k],
            in_rows(y_next if way == 0 else y_prev, z),
        )

    for way in range(2):
        for i in range(8):
            far_out[way, i] = zbuf[lax.rem(wanted(y_far, 8 * way + i), 128)]
        far_copy(way).start()
    for way in range(2):
        k = 1 - way
        for i in range(8):
            u = 8 * k + i
            near_out[way, u] = zbuf[lax.rem(wanted(y_next if way == 0 else y_prev, u), 128)]
        near_copy(way, k).start()
    for way in range(2):
        far_copy(way).wait_recv()
        for i in range(8):
            u = 8 * way + i
            block = wanted(y_next if way == 0 else y_prev, u)
            here = block // 128 == y
            near_out[way, u] = jnp.where(here, zbuf[lax.rem(block, 128)], far_in[way, i])
        near_copy(way, way).start()

    for way in range(2):
        near_copy(way, 1 - way).wait_recv()
    for way in range(2):
        near_copy(way, way).wait_recv()

    def use(u):
        block = wanted(y, u)
        ahead = lax.rem(block // 128 - y + Y, Y)
        if u < 8:
            way = jnp.where(ahead == 1, 1, 0)
        else:
            way = jnp.where(ahead == Y - 1, 0, 1)
        return jnp.where(ahead == 0, zbuf[lax.rem(block, 128)], near_in[way, u])

    def agg_copy(k, q, source):
        return remote(
            lhs.at[mine_a, pl.ds(pl.multiple_of(q * 128, 128), 128)],
            own_a.at[pl.ds(pl.multiple_of(source * 64, 64), 64)],
            as_.at[k - 1], ar.at[k - 1], in_rep(q),
        )

    for b in range(8):
        raw = dot(use(b), adj[b, 0], 1, 1) + dot(use(8 + b), adj[b, 1], 1, 1)
        agg = (raw * scale[b, 0:1, :]).astype(BF)
        lhs[mine_a, pl.ds(128 * b, 128)] = agg
    for k in range(1, REP):
        agg_copy(k, turn(rep, k, REP), rep).start()
    pair_a = remote(lhs.at[mine_a], lhs.at[mine_a], ps.at[1], pr.at[1], pair)
    pair_a.start()
    own_a[own_rows] = lhs[mine_a, pl.ds(pl.multiple_of(rep * 128, 128), 128)]
    later[3].wait()
    later[4].wait()
    for k in range(1, REP):
        agg_copy(k, rep, turn(rep, -k, REP)).wait_recv()

    pre = pre_self[...] + dot(own_a[...], wn[...], 0, 0)
    s = 1.0 / (1.0 + jnp.exp(-pre))
    out_ref[...] = (pre * s).astype(BF)
    g_own[...] = (cot[...].astype(F32) * (s * (1.0 + pre * (1.0 - s)))).astype(BF)

    def g_copy(k, q, source):
        return remote(
            g_own.at[:, pl.ds(pl.multiple_of(lax.rem(q, 2) * 256, 256), 256)],
            g_all.at[pl.ds(pl.multiple_of(source * 128, 128), 128)],
            gs.at[k - 1], gr.at[k - 1], in_rep(q),
        )

    for k in (4, 3, 5, 2, 6, 1, 7):
        g_copy(k, turn(rep, k, REP), rep).start()
    g_all[pl.ds(pl.multiple_of(rep * 128, 128), 128)] = g_own[
        :, pl.ds(pl.multiple_of(core * 256, 256), 256)
    ]
    other = pl.ds(pl.multiple_of(64 - core * 64, 64), 64)
    other_a = pl.ds(pl.multiple_of(192 - core * 64, 64), 64)
    remote(lhs.at[other], lhs.at[other], ps.at[0], pr.at[0], pair).wait_recv()
    remote(lhs.at[other_a], lhs.at[other_a], ps.at[1], pr.at[1], pair).wait_recv()
    for k in range(1, REP):
        g_copy(k, rep, turn(rep, -k, REP)).wait_recv()
    grad = dot(lhs[...], g_all[...], 1, 0)
    for q in range(4):
        cols = slice(64 * q, 64 * q + 64)
        parts[q] = jnp.concatenate([grad[:128, cols], grad[128:, cols]], axis=1)

    def part_copy(k, source):
        yy = turn(y, k, Y)
        return remote(
            parts.at[yy], y_in.at[source], ts.at[k - 1], tr.at[k - 1], in_rows(yy, z)
        )

    for k in (2, 1, 3):
        part_copy(k, y).start()
    total = parts[y]
    for k in range(1, Y):
        source = turn(y, -k, Y)
        part_copy(k, source).wait_recv()
        total = total + y_in[source]
    y_sum[...] = total.reshape(Z, 8, 128)

    def is_self(a):
        return jnp.logical_and(x * Z + a == row, 4 * core + y == rep)

    def last_copy(a, source):
        return remote(
            y_sum.at[a], z_in.at[source], us.at[a], ur.at[source],
            {"rows": x * Z + a, "rep": 4 * core + y},
        )

    def send_last(a, carry):
        @pl.when(is_self(a))
        def _():
            pltpu.make_async_copy(y_sum.at[a], z_in.at[z], ur.at[z]).start()

        @pl.when(jnp.logical_not(is_self(a)))
        def _():
            last_copy(a, z).start()

        return carry

    lax.fori_loop(0, Z, send_last, 0)

    for c in [pair_f, pair_a]:
        c.wait_send()
    for k in range(1, REP):
        feature_copy(k, turn(rep, k, REP), rep).wait_send()
        agg_copy(k, turn(rep, k, REP), rep).wait_send()
        g_copy(k, turn(rep, k, REP), rep).wait_send()
    for k in range(1, Y):
        nb_copy(k, y).wait_send()
        part_copy(k, y).wait_send()
    for way in range(2):
        far_copy(way).wait_send()
        for k in range(2):
            near_copy(way, k).wait_send()

    def ring_left(step, carry):
        for piece in range(SUB):
            for way in range(2):
                sent(way, step, piece).wait_send()
        return carry

    lax.fori_loop(0, HALF - 1, ring_left, 0)
    for piece in range(SUB):
        sent(last_way(piece), HALF - 1, piece).wait_send()

    def wait_last(a, carry):
        @pl.when(jnp.logical_not(is_self(a)))
        def _():
            last_copy(a, z).wait_send()

        last_copy(a, a).wait_recv()
        return carry

    lax.fori_loop(0, Z, wait_last, 0)
    grads = z_in[0]
    for a in range(1, Z):
        grads = grads + z_in[a]
    wg_ref[0] = grads[:, :64]
    wg_ref[1] = grads[:, 64:]


def local(features, neighbor_blocks, adjacency, w_self, w_neigh, cotangent):
    vmem, anywhere = pl.BlockSpec(memory_space=pltpu.VMEM), pl.BlockSpec(memory_space=pl.ANY)
    dma = pltpu.SemaphoreType.DMA
    return pl.pallas_call(
        kernel,
        out_shape=(
            jax.ShapeDtypeStruct((128, 512), BF),
            jax.ShapeDtypeStruct((2, 8, 64), F32),
        ),
        in_specs=[vmem] + [anywhere] * 5,
        out_specs=(vmem, vmem),
        scratch_shapes=[
            pltpu.VMEM((128, 64, 128), BF),
            pltpu.VMEM((2, 8, 64, 128), BF),
            pltpu.VMEM((2, 8, 64, 128), BF),
            pltpu.VMEM((2, 16, 64, 128), BF),
            pltpu.VMEM((2, 16, 64, 128), BF),
            pltpu.VMEM((512, 128), BF),
            pltpu.VMEM((512, 128), BF),
            pltpu.VMEM((256, 1024), BF),
            pltpu.VMEM((8, 2, 128, 128), BF),
            pltpu.VMEM((512, 512), BF),
            pltpu.VMEM((512, 512), BF),
            pltpu.VMEM((128, 512), BF),
            pltpu.VMEM((8, 8, 128), F32),
            pltpu.VMEM((128, 512), F32),
            pltpu.VMEM((128, 512), BF),
            pltpu.VMEM((1024, 256), BF),
            pltpu.VMEM((4, 128, 128), F32),
            pltpu.VMEM((4, 128, 128), F32),
            pltpu.VMEM((16, 8, 128), F32),
            pltpu.VMEM((16, 8, 128), F32),
            pltpu.VMEM((4, 2, 8), jnp.int32),
            pltpu.SMEM((4, 2, 8), jnp.int32),
            dma((14,)),
            dma((2, HALF, SUB)), dma((2, HALF, SUB)),
            dma((9,)), dma((9,)),
            dma((7,)), dma((7,)),
            dma((7,)), dma((7,)),
            dma((2,)), dma((2,)),
            dma((3,)), dma((3,)),
            dma((2, 2)), dma((2, 2)),
            dma((3,)), dma((3,)),
            dma((16,)), dma((16,)),
        ],
        compiler_params=pltpu.CompilerParams(
            collective_id=0, has_side_effects=True, vmem_limit_bytes=32 * 1024 * 1024
        ),
        cost_estimate=pl.CostEstimate(
            flops=500_000_000, bytes_accessed=2_500_000, transcendentals=65536
        ),
    )(neighbor_blocks.T, features.T, adjacency, w_self, w_neigh, cotangent)


def solution(mesh):
    in_specs = (
        P("rows", "rep"),
        P("rows", None),
        P("rows", None, None, None),
        P(),
        P(),
        P(("rows", "rep"), None),
    )
    out_specs = (P(("rows", "rep"), None), P(None, "rows", "rep"))
    return jax.shard_map(local, mesh=mesh, in_specs=in_specs, out_specs=out_specs, check_vma=False)
```

```python
import jax
import jax.numpy as jnp
from jax import lax
from jax.experimental import pallas as pl
from jax.experimental.pallas import tpu as pltpu
from jax.sharding import PartitionSpec as P

Y, Z, X = 4, 16, 4
REP = 2 * X
SUB = 4
PIECE = 8 // SUB
HALF = Z // 2
MESH = pl.DeviceIdType.MESH
BF, F32 = jnp.bfloat16, jnp.float32


def dot(a, b, ca, cb):
    return lax.dot_general(a, b, (((ca,), (cb,)), ((), ())), preferred_element_type=F32)


def kernel(
    nb_ref, f_hbm, adj_hbm, ws_hbm, wn_hbm, cot_hbm,
    out_ref, wg_ref,
    zbuf, hold, picked, used, own_f, own_a, lhs, adj, ws, wn, cot,
    scale, pre_self, g_own, g_all, parts, y_in, y_sum, z_in, table, asked, nb_s, table_s, asked_s,
    load_sem, zs, zr, fs, fr, as_, ar, gs, gr, ps, pr, ns, nr, ys, yr, ts, tr, us, ur,
):
    row, rep = lax.axis_index("rows"), lax.axis_index("rep")
    y, z = row // Z, lax.rem(row, Z)
    x, core = rep // 2, lax.rem(rep, 2)

    def in_rows(yy, zz):
        return {"rows": yy * Z + zz, "rep": rep}

    def in_rep(q):
        return {"rows": row, "rep": q}

    def remote(src, dst, send, recv, device):
        return pltpu.make_async_remote_copy(
            src_ref=src, dst_ref=dst, send_sem=send, recv_sem=recv,
            device_id=device, device_id_type=MESH,
        )

    def turn(a, k, n):
        return lax.rem(a + k + n, n)

    right, left = in_rows(y, turn(z, 1, Z)), in_rows(y, turn(z, -1, Z))

    ends = []

    def go(copy):
        copy.start()
        ends.append(copy.wait_send)

    def finish():
        for end in ends:
            end()
        ends.clear()

    first = [
        pltpu.make_async_copy(
            f_hbm.at[:, pl.ds(128 * l, 128)], zbuf.at[z * 8 + l], load_sem.at[l]
        )
        for l in range(8)
    ]
    mine = pl.ds(pl.multiple_of(core * 64, 64), 64)
    mine_a = pl.ds(pl.multiple_of(128 + core * 64, 64), 64)
    later = [
        pltpu.make_async_copy(f_hbm, lhs.at[mine], load_sem.at[8]),
        pltpu.make_async_copy(adj_hbm, adj, load_sem.at[9]),
        pltpu.make_async_copy(ws_hbm, ws, load_sem.at[10]),
        pltpu.make_async_copy(wn_hbm, wn, load_sem.at[11]),
        pltpu.make_async_copy(cot_hbm, cot, load_sem.at[12]),
    ]
    for c in first + later:
        c.start()

    barrier = pltpu.get_barrier_semaphore()
    for device in (right, left):
        pl.semaphore_signal(barrier, inc=1, device_id=device, device_id_type=MESH)
    for k in range(1, Y):
        pl.semaphore_signal(
            barrier, inc=1, device_id=in_rows(turn(y, k, Y), z), device_id_type=MESH
        )
    for k in range(1, REP):
        pl.semaphore_signal(
            barrier, inc=1, device_id=in_rep(turn(rep, k, REP)), device_id_type=MESH
        )
    owner_id = lax.broadcasted_iota(jnp.int32, (64, 8), 0)
    lane = lax.broadcasted_iota(jnp.int32, (64, 8), 1)
    low = jnp.full((64, 1), 255, jnp.int32)
    high = jnp.zeros((64, 1), jnp.int32)
    for k in range(2):
        block = nb_ref[k : k + 1, :]
        named = block // 8 == owner_id
        code = (8 * k + lane) * 8 + block % 8
        low = jnp.minimum(low, jnp.min(jnp.where(named, code, 255), axis=1, keepdims=True))
        high = jnp.maximum(high, jnp.max(jnp.where(named, code, 0), axis=1, keepdims=True))
    lane = lax.broadcasted_iota(jnp.int32, (64, 128), 1)
    table[...] = jnp.where(lane == 0, low % 8, jnp.where(lane == 1, high % 8, low // 8))
    to_smem = [
        pltpu.make_async_copy(nb_ref, nb_s, load_sem.at[13]),
        pltpu.make_async_copy(table, table_s, load_sem.at[14]),
    ]
    for c in to_smem:
        c.start()
    for c in first:
        c.wait()
    pl.semaphore_wait(barrier, 2 + (Y - 1) + (REP - 1))

    def table_copy(k):
        yy = turn(y, k, Y)
        return remote(
            table.at[pl.ds(yy * Z, Z)], asked.at[Y - k - 1], ns.at[k - 1], nr.at[k - 1],
            in_rows(yy, z),
        )

    for k in (2, 1, 3):
        go(table_copy(k))

    def ring_copy(way, step, piece, chunk):
        at = pl.ds(chunk * 8 + piece * PIECE, PIECE)
        return remote(
            zbuf.at[at], zbuf.at[at], zs.at[way, step, piece], zr.at[way, step, piece],
            right if way == 0 else left,
        )

    def sent(way, step, piece):
        return ring_copy(way, step, piece, turn(z, -step if way == 0 else step, Z))

    def arriving(way, step, piece):
        return ring_copy(way, step, piece, turn(z, -1 - step if way == 0 else 1 + step, Z))

    def last_way(piece):
        return 0 if piece < SUB // 2 else 1

    for piece in range(SUB):
        for way in range(2):
            sent(way, 0, piece).start()

    def feature_copy(k, q, source):
        return remote(
            zbuf.at[z * 8 + q], own_f.at[pl.ds(pl.multiple_of(source * 64, 64), 64)],
            fs.at[k - 1], fr.at[k - 1], in_rep(q),
        )

    for k in range(1, REP):
        go(feature_copy(k, turn(rep, k, REP), rep))
    later[0].wait()
    pair = in_rep(x * 2 + 1 - core)
    pair_f = remote(lhs.at[mine], lhs.at[mine], ps.at[0], pr.at[0], pair)
    go(pair_f)
    own_rows = pl.ds(pl.multiple_of(rep * 64, 64), 64)
    own_f[own_rows] = zbuf[z * 8 + rep]

    for k in range(1, Y):
        table_copy(k).wait_recv()
    ask_smem = pltpu.make_async_copy(asked, asked_s, load_sem.at[15])
    ask_smem.start()

    def use_copy(k, chunk):
        return remote(
            picked.at[k - 1, chunk], used.at[Y - k - 1, chunk],
            ys.at[k - 1, chunk], yr.at[Y - k - 1, chunk], in_rows(turn(y, k, Y), z),
        )

    def send_uses(chunk):
        hold[...] = zbuf[pl.ds(chunk * 8, 8)]
        for k in (2, 1, 3):
            for rank in range(2):
                picked[k - 1, chunk, rank] = hold[asked_s[k - 1, chunk, rank]]
            use_copy(k, chunk).start()

    ask_smem.wait()
    send_uses(z)

    def ring_step(step, carry):
        for piece in range(SUB):
            for way in range(2):
                arriving(way, step - 1, piece).wait_recv()
                sent(way, step, piece).start()
        for way in range(2):
            send_uses(turn(z, -step if way == 0 else step, Z))
        return carry

    lax.fori_loop(1, HALF - 1, ring_step, 0)
    for piece in range(SUB):
        for way in range(2):
            arriving(way, HALF - 2, piece).wait_recv()
            if way == last_way(piece):
                sent(way, HALF - 1, piece).start()
    for way in range(2):
        send_uses(turn(z, 1 - HALF if way == 0 else HALF - 1, Z))
    for piece in range(SUB):
        arriving(last_way(piece), HALF - 1, piece).wait_recv()
    send_uses(turn(z, HALF, Z))

    def ring_left(step, carry):
        for piece in range(SUB):
            for way in range(2):
                sent(way, step, piece).wait_send()
        return carry

    def ring_end():
        lax.fori_loop(0, HALF - 1, ring_left, 0)
        for piece in range(SUB):
            sent(last_way(piece), HALF - 1, piece).wait_send()

    ends.append(ring_end)

    def used_here(chunk, carry):
        for k in range(1, Y):
            use_copy(k, chunk).wait_recv()
        return carry

    def uses_left(chunk, carry):
        for k in range(1, Y):
            use_copy(k, chunk).wait_send()
        return carry

    ends.append(lambda: lax.fori_loop(0, Z, uses_left, 0))
    later[1].wait()
    ones = jnp.ones((8, 128), BF)
    for b in range(8):
        total = dot(ones, adj[b, 0], 1, 1) + dot(ones, adj[b, 1], 1, 1)
        scale[b] = 1.0 / jnp.sqrt(1.0 + total)
    for c in to_smem:
        c.wait()
    for k in range(1, REP):
        feature_copy(k, rep, turn(rep, -k, REP)).wait_recv()
    later[2].wait()
    pre_self[...] = dot(own_f[...], ws[...], 0, 0)
    lax.fori_loop(0, Z, used_here, 0)
    def use(u):
        block = nb_s[u // 8, u % 8]
        owner = block // 8
        ahead = lax.rem(owner // Z - y + Y, Y)
        rank = jnp.where(table_s[owner, 2] == u, 0, 1)
        other = used[jnp.maximum(ahead, 1) - 1, lax.rem(owner, Z), rank]
        return jnp.where(ahead == 0, zbuf[lax.rem(block, 8 * Z)], other)

    def agg_copy(k, q, source):
        return remote(
            lhs.at[mine_a, pl.ds(pl.multiple_of(q * 128, 128), 128)],
            own_a.at[pl.ds(pl.multiple_of(source * 64, 64), 64)],
            as_.at[k - 1], ar.at[k - 1], in_rep(q),
        )

    for b in range(8):
        raw = dot(use(b), adj[b, 0], 1, 1) + dot(use(8 + b), adj[b, 1], 1, 1)
        agg = (raw * scale[b, 0:1, :]).astype(BF)
        lhs[mine_a, pl.ds(128 * b, 128)] = agg
    for k in range(1, REP):
        go(agg_copy(k, turn(rep, k, REP), rep))
    pair_a = remote(lhs.at[mine_a], lhs.at[mine_a], ps.at[1], pr.at[1], pair)
    go(pair_a)
    finish()
    own_a[own_rows] = lhs[mine_a, pl.ds(pl.multiple_of(rep * 128, 128), 128)]
    later[3].wait()
    later[4].wait()
    for k in range(1, REP):
        agg_copy(k, rep, turn(rep, -k, REP)).wait_recv()

    pre = pre_self[...] + dot(own_a[...], wn[...], 0, 0)
    s = 1.0 / (1.0 + jnp.exp(-pre))
    out_ref[...] = (pre * s).astype(BF)
    g_own[...] = (cot[...].astype(F32) * (s * (1.0 + pre * (1.0 - s)))).astype(BF)


    def g_copy(k, q, source):
        return remote(
            g_own.at[:, pl.ds(pl.multiple_of(lax.rem(q, 2) * 256, 256), 256)],
            g_all.at[pl.ds(pl.multiple_of(source * 128, 128), 128)],
            gs.at[k - 1], gr.at[k - 1], in_rep(q),
        )

    for k in (4, 3, 5, 2, 6, 1, 7):
        go(g_copy(k, turn(rep, k, REP), rep))
    g_all[pl.ds(pl.multiple_of(rep * 128, 128), 128)] = g_own[
        :, pl.ds(pl.multiple_of(core * 256, 256), 256)
    ]
    finish()
    other = pl.ds(pl.multiple_of(64 - core * 64, 64), 64)
    other_a = pl.ds(pl.multiple_of(192 - core * 64, 64), 64)
    remote(lhs.at[other], lhs.at[other], ps.at[0], pr.at[0], pair).wait_recv()
    remote(lhs.at[other_a], lhs.at[other_a], ps.at[1], pr.at[1], pair).wait_recv()
    for k in range(1, REP):
        g_copy(k, rep, turn(rep, -k, REP)).wait_recv()
    grad = dot(lhs[...], g_all[...], 1, 0)
    for q in range(4):
        cols = slice(64 * q, 64 * q + 64)
        parts[q] = jnp.concatenate([grad[:128, cols], grad[128:, cols]], axis=1)

    def part_copy(k, source):
        yy = turn(y, k, Y)
        return remote(
            parts.at[yy], y_in.at[source], ts.at[k - 1], tr.at[k - 1], in_rows(yy, z)
        )

    for k in (2, 1, 3):
        go(part_copy(k, y))
    total = parts[y]
    for k in range(1, Y):
        source = turn(y, -k, Y)
        part_copy(k, source).wait_recv()
        total = total + y_in[source]
    y_sum[...] = total.reshape(Z, 8, 128)

    def last_copy(j, source):
        a = turn(z, j, Z)
        return remote(
            y_sum.at[a], z_in.at[source], us.at[j], ur.at[j],
            {"rows": x * Z + a, "rep": 4 * core + y},
        )

    kept = jnp.logical_and(x == y, 4 * core + y == rep)
    keep = pltpu.make_async_copy(y_sum.at[z], z_in.at[z], ur.at[0])
    for j in (8, 7, 9, 6, 10, 5, 11, 4, 12, 3, 13, 2, 14, 1, 15):
        last_copy(j, z).start()

    @pl.when(kept)
    def _():
        keep.start()

    @pl.when(jnp.logical_not(kept))
    def _():
        last_copy(0, z).start()

    finish()
    for j in range(Z):
        last_copy(j, turn(z, -j, Z)).wait_recv()
    grads = z_in[0]
    for a in range(1, Z):
        grads = grads + z_in[a]
    wg_ref[0] = grads[:, :64]
    wg_ref[1] = grads[:, 64:]
    for j in range(1, Z):
        last_copy(j, z).wait_send()

    @pl.when(jnp.logical_not(kept))
    def _():
        last_copy(0, z).wait_send()


def local(features, neighbor_blocks, adjacency, w_self, w_neigh, cotangent):
    vmem, anywhere = pl.BlockSpec(memory_space=pltpu.VMEM), pl.BlockSpec(memory_space=pl.ANY)
    dma = pltpu.SemaphoreType.DMA
    return pl.pallas_call(
        kernel,
        out_shape=(
            jax.ShapeDtypeStruct((128, 512), BF),
            jax.ShapeDtypeStruct((2, 8, 64), F32),
        ),
        in_specs=[vmem] + [anywhere] * 5,
        out_specs=(vmem, vmem),
        scratch_shapes=[
            pltpu.VMEM((128, 64, 128), BF),
            pltpu.VMEM((8, 64, 128), BF),
            pltpu.VMEM((3, 16, 2, 64, 128), BF),
            pltpu.VMEM((3, 16, 2, 64, 128), BF),
            pltpu.VMEM((512, 128), BF),
            pltpu.VMEM((512, 128), BF),
            pltpu.VMEM((256, 1024), BF),
            pltpu.VMEM((8, 2, 128, 128), BF),
            pltpu.VMEM((512, 512), BF),
            pltpu.VMEM((512, 512), BF),
            pltpu.VMEM((128, 512), BF),
            pltpu.VMEM((8, 8, 128), F32),
            pltpu.VMEM((128, 512), F32),
            pltpu.VMEM((128, 512), BF),
            pltpu.VMEM((1024, 256), BF),
            pltpu.VMEM((4, 128, 128), F32),
            pltpu.VMEM((4, 128, 128), F32),
            pltpu.VMEM((16, 8, 128), F32),
            pltpu.VMEM((16, 8, 128), F32),
            pltpu.VMEM((64, 128), jnp.int32),
            pltpu.VMEM((3, 16, 128), jnp.int32),
            pltpu.SMEM((2, 8), jnp.int32),
            pltpu.SMEM((64, 128), jnp.int32),
            pltpu.SMEM((3, 16, 128), jnp.int32),
            dma((16,)),
            dma((2, HALF, SUB)), dma((2, HALF, SUB)),
            dma((7,)), dma((7,)),
            dma((7,)), dma((7,)),
            dma((7,)), dma((7,)),
            dma((2,)), dma((2,)),
            dma((3,)), dma((3,)),
            dma((3, 16)), dma((3, 16)),
            dma((3,)), dma((3,)),
            dma((16,)), dma((16,)),
        ],
        compiler_params=pltpu.CompilerParams(
            collective_id=0, has_side_effects=True, vmem_limit_bytes=60 * 1024 * 1024
        ),
        cost_estimate=pl.CostEstimate(
            flops=500_000_000, bytes_accessed=2_500_000, transcendentals=65536
        ),
    )(neighbor_blocks.T, features.T, adjacency, w_self, w_neigh, cotangent)


def solution(mesh):
    in_specs = (
        P("rows", "rep"),
        P("rows", None),
        P("rows", None, None, None),
        P(),
        P(),
        P(("rows", "rep"), None),
    )
    out_specs = (P(("rows", "rep"), None), P(None, "rows", "rep"))
    return jax.shard_map(local, mesh=mesh, in_specs=in_specs, out_specs=out_specs, check_vma=False)
```

```python
import jax
import jax.numpy as jnp
from jax import lax
from jax.experimental import pallas as pl
from jax.experimental.pallas import tpu as pltpu
from jax.sharding import PartitionSpec as P

Y, Z, X = 4, 16, 4
REP = 2 * X
SUB = 4
PIECE = 8 // SUB
HALF = Z // 2
MESH = pl.DeviceIdType.MESH
BF, F32 = jnp.bfloat16, jnp.float32


def dot(a, b, ca, cb):
    return lax.dot_general(a, b, (((ca,), (cb,)), ((), ())), preferred_element_type=F32)


def kernel(
    nb_ref, f_hbm, adj_hbm, ws_hbm, wn_hbm, cot_hbm,
    out_ref, wg_ref,
    zbuf, hold, picked, used, own_f, own_a, lhs, adj, ws, wn, cot,
    scale, pre_self, g_own, g_all, parts, y_in, y_sum, z_in, table, asked, nb_s, table_s, asked_s,
    load_sem, zs, zr, fs, fr, as_, ar, gs, gr, ps, pr, ns, nr, ys, yr, ts, tr, us, ur,
):
    row, rep = lax.axis_index("rows"), lax.axis_index("rep")
    y, z = row // Z, lax.rem(row, Z)
    x, core = rep // 2, lax.rem(rep, 2)

    def in_rows(yy, zz):
        return {"rows": yy * Z + zz, "rep": rep}

    def in_rep(q):
        return {"rows": row, "rep": q}

    def remote(src, dst, send, recv, device):
        return pltpu.make_async_remote_copy(
            src_ref=src, dst_ref=dst, send_sem=send, recv_sem=recv,
            device_id=device, device_id_type=MESH,
        )

    def turn(a, k, n):
        return lax.rem(a + k + n, n)

    right, left = in_rows(y, turn(z, 1, Z)), in_rows(y, turn(z, -1, Z))

    ends = []

    def go(copy):
        copy.start()
        ends.append(copy.wait_send)

    def finish():
        for end in ends:
            end()
        ends.clear()

    first = [
        pltpu.make_async_copy(
            f_hbm.at[:, pl.ds(128 * l, 128)], zbuf.at[z * 8 + l], load_sem.at[l]
        )
        for l in range(8)
    ]
    mine = pl.ds(pl.multiple_of(core * 64, 64), 64)
    mine_a = pl.ds(pl.multiple_of(128 + core * 64, 64), 64)
    later = [
        pltpu.make_async_copy(f_hbm, lhs.at[mine], load_sem.at[8]),
        pltpu.make_async_copy(adj_hbm, adj, load_sem.at[9]),
        pltpu.make_async_copy(ws_hbm, ws, load_sem.at[10]),
        pltpu.make_async_copy(wn_hbm, wn, load_sem.at[11]),
        pltpu.make_async_copy(cot_hbm, cot, load_sem.at[12]),
    ]
    for c in first + later:
        c.start()

    barrier = pltpu.get_barrier_semaphore()
    for device in (right, left):
        pl.semaphore_signal(barrier, inc=1, device_id=device, device_id_type=MESH)
    for k in range(1, Y):
        pl.semaphore_signal(
            barrier, inc=1, device_id=in_rows(turn(y, k, Y), z), device_id_type=MESH
        )
    for k in range(1, REP):
        pl.semaphore_signal(
            barrier, inc=1, device_id=in_rep(turn(rep, k, REP)), device_id_type=MESH
        )
    owner_id = lax.broadcasted_iota(jnp.int32, (64, 8), 0)
    lane = lax.broadcasted_iota(jnp.int32, (64, 8), 1)
    low = jnp.full((64, 1), 255, jnp.int32)
    high = jnp.zeros((64, 1), jnp.int32)
    for k in range(2):
        block = nb_ref[k : k + 1, :]
        named = block // 8 == owner_id
        code = (8 * k + lane) * 8 + block % 8
        low = jnp.minimum(low, jnp.min(jnp.where(named, code, 255), axis=1, keepdims=True))
        high = jnp.maximum(high, jnp.max(jnp.where(named, code, 0), axis=1, keepdims=True))
    lane = lax.broadcasted_iota(jnp.int32, (64, 128), 1)
    table[...] = jnp.where(lane == 0, low % 8, jnp.where(lane == 1, high % 8, low // 8))
    to_smem = [
        pltpu.make_async_copy(nb_ref, nb_s, load_sem.at[13]),
        pltpu.make_async_copy(table, table_s, load_sem.at[14]),
    ]
    for c in to_smem:
        c.start()
    for c in first:
        c.wait()
    pl.semaphore_wait(barrier, 2 + (Y - 1) + (REP - 1))

    def table_copy(k):
        yy = turn(y, k, Y)
        return remote(
            table.at[pl.ds(yy * Z, Z)], asked.at[Y - k - 1], ns.at[k - 1], nr.at[k - 1],
            in_rows(yy, z),
        )

    for k in (2, 1, 3):
        go(table_copy(k))

    def ring_copy(way, step, piece, chunk):
        at = pl.ds(chunk * 8 + piece * PIECE, PIECE)
        return remote(
            zbuf.at[at], zbuf.at[at], zs.at[way], zr.at[way, step, piece],
            right if way == 0 else left,
        )

    def sent(way, step, piece):
        return ring_copy(way, step, piece, turn(z, -step if way == 0 else step, Z))

    def arriving(way, step, piece):
        return ring_copy(way, step, piece, turn(z, -1 - step if way == 0 else 1 + step, Z))

    def last_way(piece):
        return 0 if piece < SUB // 2 else 1

    for piece in range(SUB):
        for way in range(2):
            sent(way, 0, piece).start()

    def feature_copy(k, q, source):
        return remote(
            zbuf.at[z * 8 + q], own_f.at[pl.ds(pl.multiple_of(source * 64, 64), 64)],
            fs.at[0], fr.at[0], in_rep(q),
        )

    for k in range(1, REP):
        feature_copy(k, turn(rep, k, REP), rep).start()
    some_f = own_f.at[pl.ds(0, 448)]
    all_f = remote(some_f, some_f, fs.at[0], fr.at[0], in_rep(turn(rep, 1, REP)))
    ends.append(all_f.wait_send)
    later[0].wait()
    pair = in_rep(x * 2 + 1 - core)
    pair_f = remote(lhs.at[mine], lhs.at[mine], ps.at[0], pr.at[0], pair)
    go(pair_f)
    own_rows = pl.ds(pl.multiple_of(rep * 64, 64), 64)
    own_f[own_rows] = zbuf[z * 8 + rep]

    for k in range(1, Y):
        table_copy(k).wait_recv()
    ask_smem = pltpu.make_async_copy(asked, asked_s, load_sem.at[15])
    ask_smem.start()

    def use_copy(k, chunk):
        return remote(
            picked.at[k - 1, chunk], used.at[Y - k - 1, chunk],
            ys.at[k - 1], yr.at[Y - k - 1], in_rows(turn(y, k, Y), z),
        )

    def send_uses(chunk):
        hold[...] = zbuf[pl.ds(chunk * 8, 8)]
        for k in (2, 1, 3):
            for rank in range(2):
                picked[k - 1, chunk, rank] = hold[asked_s[k - 1, chunk, rank]]
            use_copy(k, chunk).start()

    ask_smem.wait()
    send_uses(z)

    def ring_step(step, carry):
        for piece in range(SUB):
            for way in range(2):
                arriving(way, step - 1, piece).wait_recv()
                sent(way, step, piece).start()
        for way in range(2):
            send_uses(turn(z, -step if way == 0 else step, Z))
        return carry

    lax.fori_loop(1, HALF - 1, ring_step, 0)
    for piece in range(SUB):
        for way in range(2):
            arriving(way, HALF - 2, piece).wait_recv()
            if way == last_way(piece):
                sent(way, HALF - 1, piece).start()
    for way in range(2):
        send_uses(turn(z, 1 - HALF if way == 0 else HALF - 1, Z))
    for piece in range(SUB):
        arriving(last_way(piece), HALF - 1, piece).wait_recv()
    send_uses(turn(z, HALF, Z))

    def ring_end():
        for way in range(2):
            all_sent = zbuf.at[pl.ds(0, 8 * HALF - 4)]
            remote(all_sent, all_sent, zs.at[way], zr.at[way, 0, 0], right).wait_send()

    ends.append(ring_end)

    def all_uses(k):
        return remote(
            picked.at[k - 1], used.at[Y - k - 1], ys.at[k - 1], yr.at[Y - k - 1],
            in_rows(turn(y, k, Y), z),
        )

    def uses_left():
        for k in range(1, Y):
            all_uses(k).wait_send()

    ends.append(uses_left)
    later[1].wait()
    ones = jnp.ones((8, 128), BF)
    for b in range(8):
        total = dot(ones, adj[b, 0], 1, 1) + dot(ones, adj[b, 1], 1, 1)
        scale[b] = 1.0 / jnp.sqrt(1.0 + total)
    for c in to_smem:
        c.wait()
    all_f.wait_recv()
    later[2].wait()
    pre_self[...] = dot(own_f[...], ws[...], 0, 0)
    for k in range(1, Y):
        all_uses(k).wait_recv()
    def use(u):
        block = nb_s[u // 8, u % 8]
        owner = block // 8
        ahead = lax.rem(owner // Z - y + Y, Y)
        rank = jnp.where(table_s[owner, 2] == u, 0, 1)
        other = used[jnp.maximum(ahead, 1) - 1, lax.rem(owner, Z), rank]
        return jnp.where(ahead == 0, zbuf[lax.rem(block, 8 * Z)], other)

    def agg_copy(k, q, source):
        return remote(
            lhs.at[mine_a, pl.ds(pl.multiple_of(q * 128, 128), 128)],
            own_a.at[pl.ds(pl.multiple_of(source * 64, 64), 64)],
            as_.at[0], ar.at[0], in_rep(q),
        )

    for b in range(8):
        raw = dot(use(b), adj[b, 0], 1, 1) + dot(use(8 + b), adj[b, 1], 1, 1)
        agg = (raw * scale[b, 0:1, :]).astype(BF)
        lhs[mine_a, pl.ds(128 * b, 128)] = agg
    for k in range(1, REP):
        agg_copy(k, turn(rep, k, REP), rep).start()
    some_a = own_a.at[pl.ds(0, 448)]
    all_a = remote(some_a, some_a, as_.at[0], ar.at[0], in_rep(turn(rep, 1, REP)))
    pair_a = remote(lhs.at[mine_a], lhs.at[mine_a], ps.at[1], pr.at[1], pair)
    go(pair_a)
    finish()
    own_a[own_rows] = lhs[mine_a, pl.ds(pl.multiple_of(rep * 128, 128), 128)]
    later[3].wait()
    later[4].wait()
    all_a.wait_recv()
    ends.append(all_a.wait_send)

    pre = pre_self[...] + dot(own_a[...], wn[...], 0, 0)
    s = 1.0 / (1.0 + jnp.exp(-pre))
    out_ref[...] = (pre * s).astype(BF)
    g_own[...] = (cot[...].astype(F32) * (s * (1.0 + pre * (1.0 - s)))).astype(BF)


    def g_copy(k, q, source):
        return remote(
            g_own.at[:, pl.ds(pl.multiple_of(lax.rem(q, 2) * 256, 256), 256)],
            g_all.at[pl.ds(pl.multiple_of(source * 128, 128), 128)],
            gs.at[0], gr.at[0], in_rep(q),
        )

    for k in (4, 3, 5, 2, 6, 1, 7):
        g_copy(k, turn(rep, k, REP), rep).start()
    some_g = g_all.at[pl.ds(0, 896)]
    all_g = remote(some_g, some_g, gs.at[0], gr.at[0], in_rep(turn(rep, 1, REP)))
    g_all[pl.ds(pl.multiple_of(rep * 128, 128), 128)] = g_own[
        :, pl.ds(pl.multiple_of(core * 256, 256), 256)
    ]
    finish()
    other = pl.ds(pl.multiple_of(64 - core * 64, 64), 64)
    other_a = pl.ds(pl.multiple_of(192 - core * 64, 64), 64)
    remote(lhs.at[other], lhs.at[other], ps.at[0], pr.at[0], pair).wait_recv()
    remote(lhs.at[other_a], lhs.at[other_a], ps.at[1], pr.at[1], pair).wait_recv()
    all_g.wait_recv()
    ends.append(all_g.wait_send)
    grad = dot(lhs[...], g_all[...], 1, 0)
    for q in range(4):
        cols = slice(64 * q, 64 * q + 64)
        part = jnp.concatenate([grad[:128, cols], grad[128:, cols]], axis=1)
        parts[q] = part.astype(BF)

    def part_copy(q, source):
        return remote(
            parts.at[q], y_in.at[source], ts.at[q], tr.at[source],
            {"rows": x * Z + z, "rep": 4 * core + q},
        )

    def part_stays(q):
        return jnp.logical_and(x == y, 4 * core + q == rep)

    for q in range(4):
        keep = pltpu.make_async_copy(parts.at[q], y_in.at[y], tr.at[y])
        stays = part_stays(q)
        pl.when(stays)(keep.start)
        pl.when(jnp.logical_not(stays))(part_copy(q, y).start)
    total = jnp.zeros((128, 128), F32)
    for source in range(4):
        part_copy(0, source).wait_recv()
        total = total + y_in[source].astype(F32)
    y_sum[...] = total.reshape(Z, 8, 128)

    def last_copy(j, source):
        a = turn(z, j, Z)
        return remote(
            y_sum.at[a], z_in.at[source], us.at[0], ur.at[0], in_rows(y, a)
        )

    for j in (8, 7, 9, 6, 10, 5, 11, 4, 12, 3, 13, 2, 14, 1, 15):
        last_copy(j, z).start()
    z_in[z] = y_sum[z]
    finish()
    for q in range(4):
        pl.when(jnp.logical_not(part_stays(q)))(part_copy(q, y).wait_send)
    some_z = z_in.at[pl.ds(0, Z - 1)]
    all_z = remote(some_z, some_z, us.at[0], ur.at[0], right)
    all_z.wait_recv()
    grads = z_in[0]
    for a in range(1, Z):
        grads = grads + z_in[a]
    wg_ref[0] = grads[:, :64]
    wg_ref[1] = grads[:, 64:]
    all_z.wait_send()


def local(features, neighbor_blocks, adjacency, w_self, w_neigh, cotangent):
    vmem, anywhere = pl.BlockSpec(memory_space=pltpu.VMEM), pl.BlockSpec(memory_space=pl.ANY)
    dma = pltpu.SemaphoreType.DMA
    return pl.pallas_call(
        kernel,
        out_shape=(
            jax.ShapeDtypeStruct((128, 512), BF),
            jax.ShapeDtypeStruct((2, 8, 64), F32),
        ),
        in_specs=[vmem] + [anywhere] * 5,
        out_specs=(vmem, vmem),
        scratch_shapes=[
            pltpu.VMEM((128, 64, 128), BF),
            pltpu.VMEM((8, 64, 128), BF),
            pltpu.VMEM((3, 16, 2, 64, 128), BF),
            pltpu.VMEM((3, 16, 2, 64, 128), BF),
            pltpu.VMEM((512, 128), BF),
            pltpu.VMEM((512, 128), BF),
            pltpu.VMEM((256, 1024), BF),
            pltpu.VMEM((8, 2, 128, 128), BF),
            pltpu.VMEM((512, 512), BF),
            pltpu.VMEM((512, 512), BF),
            pltpu.VMEM((128, 512), BF),
            pltpu.VMEM((8, 8, 128), F32),
            pltpu.VMEM((128, 512), F32),
            pltpu.VMEM((128, 512), BF),
            pltpu.VMEM((1024, 256), BF),
            pltpu.VMEM((4, 128, 128), BF),
            pltpu.VMEM((4, 128, 128), BF),
            pltpu.VMEM((16, 8, 128), F32),
            pltpu.VMEM((16, 8, 128), F32),
            pltpu.VMEM((64, 128), jnp.int32),
            pltpu.VMEM((3, 16, 128), jnp.int32),
            pltpu.SMEM((2, 8), jnp.int32),
            pltpu.SMEM((64, 128), jnp.int32),
            pltpu.SMEM((3, 16, 128), jnp.int32),
            dma((16,)),
            dma((2,)), dma((2, HALF, SUB)),
            dma((1,)), dma((1,)),
            dma((1,)), dma((1,)),
            dma((1,)), dma((1,)),
            dma((2,)), dma((2,)),
            dma((3,)), dma((3,)),
            dma((3,)), dma((3,)),
            dma((4,)), dma((4,)),
            dma((1,)), dma((1,)),
        ],
        compiler_params=pltpu.CompilerParams(
            collective_id=0, has_side_effects=True, vmem_limit_bytes=60 * 1024 * 1024
        ),
        cost_estimate=pl.CostEstimate(
            flops=500_000_000, bytes_accessed=2_500_000, transcendentals=65536
        ),
    )(neighbor_blocks.T, features.T, adjacency, w_self, w_neigh, cotangent)


def solution(mesh):
    in_specs = (
        P("rows", "rep"),
        P("rows", None),
        P("rows", None, None, None),
        P(),
        P(),
        P(("rows", "rep"), None),
    )
    out_specs = (P(("rows", "rep"), None), P(None, "rows", "rep"))
    return jax.shard_map(local, mesh=mesh, in_specs=in_specs, out_specs=out_specs, check_vma=False)
```

```python
import jax
import jax.numpy as jnp
from jax import lax
from jax.experimental import pallas as pl
from jax.experimental.pallas import tpu as pltpu
from jax.sharding import PartitionSpec as P

Y, Z, X = 4, 16, 4
REP = 2 * X
SUB = 4
PIECE = 8 // SUB
HALF = Z // 2
MESH = pl.DeviceIdType.MESH
BF, F32 = jnp.bfloat16, jnp.float32


def dot(a, b, ca, cb):
    return lax.dot_general(a, b, (((ca,), (cb,)), ((), ())), preferred_element_type=F32)


def kernel(
    nb_ref, f_hbm, adj_hbm, ws_hbm, wn_hbm, cot_hbm,
    out_ref, wg_ref,
    zbuf, hold, picked, used, own_f, own_a, lhs, adj, ws, wn, cot,
    scale, pre_self, g_own, g_all, parts, y_in, y_sum, z_in, table, asked, nb_s, table_s, asked_s,
    load_sem, zs, zr, fs, fr, as_, ar, gs, gr, ps, pr, ns, nr, ys, yr, ts, tr, us, ur,
):
    row, rep = lax.axis_index("rows"), lax.axis_index("rep")
    y, z = row // Z, lax.rem(row, Z)
    x, core = rep // 2, lax.rem(rep, 2)

    def in_rows(yy, zz):
        return {"rows": yy * Z + zz, "rep": rep}

    def in_rep(q):
        return {"rows": row, "rep": q}

    def remote(src, dst, send, recv, device):
        return pltpu.make_async_remote_copy(
            src_ref=src, dst_ref=dst, send_sem=send, recv_sem=recv,
            device_id=device, device_id_type=MESH,
        )

    def turn(a, k, n):
        return lax.rem(a + k + n, n)

    right, left = in_rows(y, turn(z, 1, Z)), in_rows(y, turn(z, -1, Z))

    ends = []

    def go(copy):
        copy.start()
        ends.append(copy.wait_send)

    def finish():
        for end in ends:
            end()
        ends.clear()

    first = [
        pltpu.make_async_copy(
            f_hbm.at[:, pl.ds(128 * l, 128)], zbuf.at[z * 8 + l], load_sem.at[l]
        )
        for l in range(8)
    ]
    mine = pl.ds(pl.multiple_of(core * 64, 64), 64)
    mine_a = pl.ds(pl.multiple_of(128 + core * 64, 64), 64)
    later = [
        pltpu.make_async_copy(f_hbm, lhs.at[mine], load_sem.at[8]),
        pltpu.make_async_copy(adj_hbm, adj, load_sem.at[9]),
        pltpu.make_async_copy(ws_hbm, ws, load_sem.at[10]),
        pltpu.make_async_copy(wn_hbm, wn, load_sem.at[11]),
        pltpu.make_async_copy(cot_hbm, cot, load_sem.at[12]),
    ]
    for c in first + later:
        c.start()

    barrier = pltpu.get_barrier_semaphore()
    for device in (right, left):
        pl.semaphore_signal(barrier, inc=1, device_id=device, device_id_type=MESH)
    for k in range(1, Y):
        pl.semaphore_signal(
            barrier, inc=1, device_id=in_rows(turn(y, k, Y), z), device_id_type=MESH
        )
    for k in range(1, REP):
        pl.semaphore_signal(
            barrier, inc=1, device_id=in_rep(turn(rep, k, REP)), device_id_type=MESH
        )
    owner_id = lax.broadcasted_iota(jnp.int32, (64, 8), 0)
    lane = lax.broadcasted_iota(jnp.int32, (64, 8), 1)
    low = jnp.full((64, 1), 255, jnp.int32)
    high = jnp.zeros((64, 1), jnp.int32)
    for k in range(2):
        block = nb_ref[k : k + 1, :]
        named = block // 8 == owner_id
        code = (8 * k + lane) * 8 + block % 8
        low = jnp.minimum(low, jnp.min(jnp.where(named, code, 255), axis=1, keepdims=True))
        high = jnp.maximum(high, jnp.max(jnp.where(named, code, 0), axis=1, keepdims=True))
    lane = lax.broadcasted_iota(jnp.int32, (64, 128), 1)
    table[...] = jnp.where(lane == 0, low % 8, jnp.where(lane == 1, high % 8, low // 8))
    to_smem = [
        pltpu.make_async_copy(nb_ref, nb_s, load_sem.at[13]),
        pltpu.make_async_copy(table, table_s, load_sem.at[14]),
    ]
    for c in to_smem:
        c.start()
    for c in first:
        c.wait()
    pl.semaphore_wait(barrier, 2 + (Y - 1) + (REP - 1))

    def table_copy(k):
        yy = turn(y, k, Y)
        return remote(
            table.at[pl.ds(yy * Z, Z)], asked.at[Y - k - 1], ns.at[k - 1], nr.at[k - 1],
            in_rows(yy, z),
        )

    for k in (2, 1, 3):
        go(table_copy(k))

    def ring_copy(way, step, piece, chunk):
        at = pl.ds(chunk * 8 + piece * PIECE, PIECE)
        return remote(
            zbuf.at[at], zbuf.at[at], zs.at[way], zr.at[way, step, piece],
            right if way == 0 else left,
        )

    def sent(way, step, piece):
        return ring_copy(way, step, piece, turn(z, -step if way == 0 else step, Z))

    def arriving(way, step, piece):
        return ring_copy(way, step, piece, turn(z, -1 - step if way == 0 else 1 + step, Z))

    def last_way(piece):
        return 0 if piece < SUB // 2 else 1

    for piece in range(SUB):
        for way in range(2):
            sent(way, 0, piece).start()

    def feature_copy(k, q, source):
        return remote(
            zbuf.at[z * 8 + q], own_f.at[pl.ds(pl.multiple_of(source * 64, 64), 64)],
            fs.at[0], fr.at[0], in_rep(q),
        )

    for k in range(1, REP):
        feature_copy(k, turn(rep, k, REP), rep).start()
    some_f = own_f.at[pl.ds(0, 448)]
    all_f = remote(some_f, some_f, fs.at[0], fr.at[0], in_rep(turn(rep, 1, REP)))
    ends.append(all_f.wait_send)
    later[0].wait()
    pair = in_rep(x * 2 + 1 - core)
    pair_f = remote(lhs.at[mine], lhs.at[mine], ps.at[0], pr.at[0], pair)
    go(pair_f)
    own_rows = pl.ds(pl.multiple_of(rep * 64, 64), 64)
    own_f[own_rows] = zbuf[z * 8 + rep]

    for k in range(1, Y):
        table_copy(k).wait_recv()
    ask_smem = pltpu.make_async_copy(asked, asked_s, load_sem.at[15])
    ask_smem.start()

    def use_copy(k, chunk):
        return remote(
            picked.at[k - 1, chunk], used.at[Y - k - 1, chunk],
            ys.at[k - 1], yr.at[Y - k - 1], in_rows(turn(y, k, Y), z),
        )

    def send_uses(chunk):
        hold[...] = zbuf[pl.ds(chunk * 8, 8)]
        for k in (2, 1, 3):
            for rank in range(2):
                picked[k - 1, chunk, rank] = hold[asked_s[k - 1, chunk, rank]]
            use_copy(k, chunk).start()

    def forward(step, pieces):
        for piece in pieces:
            for way in range(2):
                arriving(way, step - 1, piece).wait_recv()
                sent(way, step, piece).start()

    forward(1, range(SUB // 2))
    ask_smem.wait()
    send_uses(z)
    forward(1, range(SUB // 2, SUB))
    for way in range(2):
        send_uses(turn(z, -1 if way == 0 else 1, Z))

    def ring_step(step, carry):
        forward(step, range(SUB))
        for way in range(2):
            send_uses(turn(z, -step if way == 0 else step, Z))
        return carry

    lax.fori_loop(2, HALF - 1, ring_step, 0)
    for piece in range(SUB):
        for way in range(2):
            arriving(way, HALF - 2, piece).wait_recv()
            if way == last_way(piece):
                sent(way, HALF - 1, piece).start()
    for way in range(2):
        send_uses(turn(z, 1 - HALF if way == 0 else HALF - 1, Z))
    for piece in range(SUB):
        arriving(last_way(piece), HALF - 1, piece).wait_recv()
    send_uses(turn(z, HALF, Z))

    def ring_end():
        for way in range(2):
            all_sent = zbuf.at[pl.ds(0, 8 * HALF - 4)]
            remote(all_sent, all_sent, zs.at[way], zr.at[way, 0, 0], right).wait_send()

    ends.append(ring_end)

    def all_uses(k):
        return remote(
            picked.at[k - 1], used.at[Y - k - 1], ys.at[k - 1], yr.at[Y - k - 1],
            in_rows(turn(y, k, Y), z),
        )

    def uses_left():
        for k in range(1, Y):
            all_uses(k).wait_send()

    ends.append(uses_left)
    later[1].wait()
    ones = jnp.ones((8, 128), BF)
    for b in range(8):
        total = dot(ones, adj[b, 0], 1, 1) + dot(ones, adj[b, 1], 1, 1)
        scale[b] = 1.0 / jnp.sqrt(1.0 + total)
    for c in to_smem:
        c.wait()
    all_f.wait_recv()
    later[2].wait()
    pre_self[...] = dot(own_f[...], ws[...], 0, 0)
    for k in range(1, Y):
        all_uses(k).wait_recv()
    def use(k, b):
        block = nb_s[k, b]
        owner = block // 8
        ahead = lax.rem(owner // Z - y + Y, Y)
        rank = jnp.where(table_s[owner, 2] == 8 * k + b, 0, 1)
        other = used[jnp.maximum(ahead, 1) - 1, lax.rem(owner, Z), rank]
        return jnp.where(ahead == 0, zbuf[lax.rem(block, 8 * Z)], other)

    def agg_copy(k, q, source):
        return remote(
            lhs.at[mine_a, pl.ds(pl.multiple_of(q * 128, 128), 128)],
            own_a.at[pl.ds(pl.multiple_of(source * 64, 64), 64)],
            as_.at[0], ar.at[0], in_rep(q),
        )

    for k in (4, 3, 5, 2, 6, 1, 7, 0):
        b = turn(rep, k, REP)
        raw = dot(use(0, b), adj[b, 0], 1, 1) + dot(use(1, b), adj[b, 1], 1, 1)
        agg = (raw * scale[b, 0:1, :]).astype(BF)
        lhs[mine_a, pl.ds(pl.multiple_of(128 * b, 128), 128)] = agg
        if k:
            agg_copy(k, b, rep).start()
        else:
            own_a[own_rows] = agg
    some_a = own_a.at[pl.ds(0, 448)]
    all_a = remote(some_a, some_a, as_.at[0], ar.at[0], in_rep(turn(rep, 1, REP)))
    pair_a = remote(lhs.at[mine_a], lhs.at[mine_a], ps.at[1], pr.at[1], pair)
    go(pair_a)
    finish()
    later[3].wait()
    later[4].wait()
    all_a.wait_recv()
    ends.append(all_a.wait_send)


    def g_copy(k, q, source):
        return remote(
            g_own.at[:, pl.ds(256 * (k % 2), 256)],
            g_all.at[pl.ds(pl.multiple_of(source * 128, 128), 128)],
            gs.at[0], gr.at[0], in_rep(q),
        )

    for half in range(2):
        cols = slice(256 * half, 256 * half + 256)
        pre = pre_self[:, cols] + dot(own_a[...], wn[:, cols], 0, 0)
        s = 1.0 / (1.0 + jnp.exp(-pre))
        g_own[:, cols] = (cot[:, cols].astype(F32) * (s * (1.0 + pre * (1.0 - s)))).astype(BF)
        out_ref[:, cols] = (pre * s).astype(BF)
        for step in (2, 1, 3):
            chip = turn(x, step, X)
            g_copy(2 * step + half, 2 * chip + half, rep).start()

        @pl.when(core != half)
        def _():
            g_copy(half, 2 * x + half, rep).start()

    some_g = g_all.at[pl.ds(0, 896)]
    all_g = remote(some_g, some_g, gs.at[0], gr.at[0], in_rep(turn(rep, 1, REP)))
    g_all[pl.ds(pl.multiple_of(rep * 128, 128), 128)] = g_own[
        :, pl.ds(pl.multiple_of(core * 256, 256), 256)
    ]
    finish()
    other = pl.ds(pl.multiple_of(64 - core * 64, 64), 64)
    other_a = pl.ds(pl.multiple_of(192 - core * 64, 64), 64)
    remote(lhs.at[other], lhs.at[other], ps.at[0], pr.at[0], pair).wait_recv()
    remote(lhs.at[other_a], lhs.at[other_a], ps.at[1], pr.at[1], pair).wait_recv()
    all_g.wait_recv()
    ends.append(all_g.wait_send)
    grad = dot(lhs[...], g_all[...], 1, 0)
    for q in range(4):
        cols = slice(64 * q, 64 * q + 64)
        part = jnp.concatenate([grad[:128, cols], grad[128:, cols]], axis=1)
        parts[q] = part.astype(BF)

    def part_copy(q, source):
        return remote(
            parts.at[q], y_in.at[source], ts.at[q], tr.at[source],
            {"rows": x * Z + z, "rep": 4 * core + q},
        )

    def part_stays(q):
        return jnp.logical_and(x == y, 4 * core + q == rep)

    for q in range(4):
        keep = pltpu.make_async_copy(parts.at[q], y_in.at[y], tr.at[y])
        stays = part_stays(q)
        pl.when(stays)(keep.start)
        pl.when(jnp.logical_not(stays))(part_copy(q, y).start)
    total = jnp.zeros((128, 128), F32)
    for source in range(4):
        part_copy(0, source).wait_recv()
        total = total + y_in[source].astype(F32)
    y_sum[...] = total.reshape(Z, 8, 128)

    def last_copy(j, source):
        a = turn(z, j, Z)
        return remote(
            y_sum.at[a], z_in.at[source], us.at[0], ur.at[0], in_rows(y, a)
        )

    for j in (8, 7, 9, 6, 10, 5, 11, 4, 12, 3, 13, 2, 14, 1, 15):
        last_copy(j, z).start()
    z_in[z] = y_sum[z]
    finish()
    for q in range(4):
        pl.when(jnp.logical_not(part_stays(q)))(part_copy(q, y).wait_send)
    some_z = z_in.at[pl.ds(0, Z - 1)]
    all_z = remote(some_z, some_z, us.at[0], ur.at[0], right)
    all_z.wait_recv()
    grads = z_in[0]
    for a in range(1, Z):
        grads = grads + z_in[a]
    wg_ref[0] = grads[:, :64]
    wg_ref[1] = grads[:, 64:]
    all_z.wait_send()


def local(features, neighbor_blocks, adjacency, w_self, w_neigh, cotangent):
    vmem, anywhere = pl.BlockSpec(memory_space=pltpu.VMEM), pl.BlockSpec(memory_space=pl.ANY)
    dma = pltpu.SemaphoreType.DMA
    return pl.pallas_call(
        kernel,
        out_shape=(
            jax.ShapeDtypeStruct((128, 512), BF),
            jax.ShapeDtypeStruct((2, 8, 64), F32),
        ),
        in_specs=[vmem] + [anywhere] * 5,
        out_specs=(vmem, vmem),
        scratch_shapes=[
            pltpu.VMEM((128, 64, 128), BF),
            pltpu.VMEM((8, 64, 128), BF),
            pltpu.VMEM((3, 16, 2, 64, 128), BF),
            pltpu.VMEM((3, 16, 2, 64, 128), BF),
            pltpu.VMEM((512, 128), BF),
            pltpu.VMEM((512, 128), BF),
            pltpu.VMEM((256, 1024), BF),
            pltpu.VMEM((8, 2, 128, 128), BF),
            pltpu.VMEM((512, 512), BF),
            pltpu.VMEM((512, 512), BF),
            pltpu.VMEM((128, 512), BF),
            pltpu.VMEM((8, 8, 128), F32),
            pltpu.VMEM((128, 512), F32),
            pltpu.VMEM((128, 512), BF),
            pltpu.VMEM((1024, 256), BF),
            pltpu.VMEM((4, 128, 128), BF),
            pltpu.VMEM((4, 128, 128), BF),
            pltpu.VMEM((16, 8, 128), F32),
            pltpu.VMEM((16, 8, 128), F32),
            pltpu.VMEM((64, 128), jnp.int32),
            pltpu.VMEM((3, 16, 128), jnp.int32),
            pltpu.SMEM((2, 8), jnp.int32),
            pltpu.SMEM((64, 128), jnp.int32),
            pltpu.SMEM((3, 16, 128), jnp.int32),
            dma((16,)),
            dma((2,)), dma((2, HALF, SUB)),
            dma((1,)), dma((1,)),
            dma((1,)), dma((1,)),
            dma((1,)), dma((1,)),
            dma((2,)), dma((2,)),
            dma((3,)), dma((3,)),
            dma((3,)), dma((3,)),
            dma((4,)), dma((4,)),
            dma((1,)), dma((1,)),
        ],
        compiler_params=pltpu.CompilerParams(
            collective_id=0, has_side_effects=True, vmem_limit_bytes=60 * 1024 * 1024
        ),
        cost_estimate=pl.CostEstimate(
            flops=500_000_000, bytes_accessed=2_500_000, transcendentals=65536
        ),
    )(neighbor_blocks.T, features.T, adjacency, w_self, w_neigh, cotangent)


def solution(mesh):
    in_specs = (
        P("rows", "rep"),
        P("rows", None),
        P("rows", None, None, None),
        P(),
        P(),
        P(("rows", "rep"), None),
    )
    out_specs = (P(("rows", "rep"), None), P(None, "rows", "rep"))
    return jax.shard_map(local, mesh=mesh, in_specs=in_specs, out_specs=out_specs, check_vma=False)
```

```python
import jax
import jax.numpy as jnp
from jax import lax
from jax.experimental import pallas as pl
from jax.experimental.pallas import tpu as pltpu
from jax.sharding import PartitionSpec as P

Y, Z, X = 4, 16, 4
REP = 2 * X
SUB = 4
PIECE = 8 // SUB
HALF = Z // 2
MESH = pl.DeviceIdType.MESH
BF, F32 = jnp.bfloat16, jnp.float32


def dot(a, b, ca, cb):
    return lax.dot_general(a, b, (((ca,), (cb,)), ((), ())), preferred_element_type=F32)


def kernel(
    nb_hbm, f_hbm, adj_hbm, ws_hbm, wn_hbm, cot_hbm,
    out_ref, wg_ref,
    zbuf, hold, picked, used, own_f, own_a, lhs, adj, ws, wn, cot,
    scale, pre_self, g_own, g_all, parts, y_in, y_sum, z_in, table, asked, nb_v, nb_s, table_s, asked_s,
    load_sem, zs, zr, fs, fr, as_, ar, gs, gr, ps, pr, ns, nr, ys, yr, ts, tr, us, ur,
):
    row, rep = lax.axis_index("rows"), lax.axis_index("rep")
    y, z = row // Z, lax.rem(row, Z)
    x, core = rep // 2, lax.rem(rep, 2)

    def in_rows(yy, zz):
        return {"rows": yy * Z + zz, "rep": rep}

    def in_rep(q):
        return {"rows": row, "rep": q}

    def remote(src, dst, send, recv, device):
        return pltpu.make_async_remote_copy(
            src_ref=src, dst_ref=dst, send_sem=send, recv_sem=recv,
            device_id=device, device_id_type=MESH,
        )

    def turn(a, k, n):
        return lax.rem(a + k + n, n)

    right, left = in_rows(y, turn(z, 1, Z)), in_rows(y, turn(z, -1, Z))

    ends = []

    def go(copy):
        copy.start()
        ends.append(copy.wait_send)

    def finish():
        for end in ends:
            end()
        ends.clear()

    first = [
        pltpu.make_async_copy(
            f_hbm.at[:, pl.ds(128 * l, 128)], zbuf.at[z * 8 + l], load_sem.at[l]
        )
        for l in range(8)
    ]
    mine = pl.ds(pl.multiple_of(core * 64, 64), 64)
    mine_a = pl.ds(pl.multiple_of(128 + core * 64, 64), 64)
    later = [
        pltpu.make_async_copy(f_hbm, lhs.at[mine], load_sem.at[8]),
        pltpu.make_async_copy(adj_hbm, adj, load_sem.at[9]),
        pltpu.make_async_copy(ws_hbm, ws, load_sem.at[10]),
        pltpu.make_async_copy(wn_hbm, wn, load_sem.at[11]),
        pltpu.make_async_copy(cot_hbm, cot, load_sem.at[12]),
    ]
    numbers = pltpu.make_async_copy(nb_hbm, nb_v, load_sem.at[16])
    numbers.start()
    for c in first:
        c.start()

    barrier = pltpu.get_barrier_semaphore()
    for device in (right, left):
        pl.semaphore_signal(barrier, inc=1, device_id=device, device_id_type=MESH)
    for k in range(1, Y):
        pl.semaphore_signal(
            barrier, inc=1, device_id=in_rows(turn(y, k, Y), z), device_id_type=MESH
        )
    for k in range(1, REP):
        pl.semaphore_signal(
            barrier, inc=1, device_id=in_rep(turn(rep, k, REP)), device_id_type=MESH
        )
    for c in later:
        c.start()
    numbers.wait()
    owner_id = lax.broadcasted_iota(jnp.int32, (64, 8), 0)
    lane = lax.broadcasted_iota(jnp.int32, (64, 8), 1)
    low = jnp.full((64, 1), 255, jnp.int32)
    high = jnp.zeros((64, 1), jnp.int32)
    for k in range(2):
        block = nb_v[k : k + 1, :]
        named = block // 8 == owner_id
        code = (8 * k + lane) * 8 + block % 8
        low = jnp.minimum(low, jnp.min(jnp.where(named, code, 255), axis=1, keepdims=True))
        high = jnp.maximum(high, jnp.max(jnp.where(named, code, 0), axis=1, keepdims=True))
    lane = lax.broadcasted_iota(jnp.int32, (64, 128), 1)
    table[...] = jnp.where(lane == 0, low % 8, jnp.where(lane == 1, high % 8, low // 8))
    to_smem = [
        pltpu.make_async_copy(nb_v, nb_s, load_sem.at[13]),
        pltpu.make_async_copy(table, table_s, load_sem.at[14]),
    ]
    for c in to_smem:
        c.start()
    for c in first:
        c.wait()
    pl.semaphore_wait(barrier, 2 + (Y - 1) + (REP - 1))

    def table_copy(k):
        yy = turn(y, k, Y)
        return remote(
            table.at[pl.ds(yy * Z, Z)], asked.at[Y - k - 1], ns.at[k - 1], nr.at[k - 1],
            in_rows(yy, z),
        )


    def ring_copy(way, step, piece, chunk):
        at = pl.ds(chunk * 8 + piece * PIECE, PIECE)
        return remote(
            zbuf.at[at], zbuf.at[at], zs.at[way], zr.at[way, step, piece],
            right if way == 0 else left,
        )

    def sent(way, step, piece):
        return ring_copy(way, step, piece, turn(z, -step if way == 0 else step, Z))

    def arriving(way, step, piece):
        return ring_copy(way, step, piece, turn(z, -1 - step if way == 0 else 1 + step, Z))

    def last_way(piece):
        return 0 if piece < SUB // 2 else 1

    for way in range(2):
        sent(way, 0, 0).start()
    for k in (2, 1, 3):
        go(table_copy(k))
    for piece in range(1, SUB):
        for way in range(2):
            sent(way, 0, piece).start()

    def feature_copy(k, q, source):
        return remote(
            zbuf.at[z * 8 + q], own_f.at[pl.ds(pl.multiple_of(source * 64, 64), 64)],
            fs.at[0], fr.at[0], in_rep(q),
        )

    for k in range(1, REP):
        feature_copy(k, turn(rep, k, REP), rep).start()
    some_f = own_f.at[pl.ds(0, 448)]
    all_f = remote(some_f, some_f, fs.at[0], fr.at[0], in_rep(turn(rep, 1, REP)))
    ends.append(all_f.wait_send)
    later[0].wait()
    pair = in_rep(x * 2 + 1 - core)
    pair_f = remote(lhs.at[mine], lhs.at[mine], ps.at[0], pr.at[0], pair)
    go(pair_f)
    own_rows = pl.ds(pl.multiple_of(rep * 64, 64), 64)
    own_f[own_rows] = zbuf[z * 8 + rep]

    for k in range(1, Y):
        table_copy(k).wait_recv()
    ask_smem = pltpu.make_async_copy(asked, asked_s, load_sem.at[15])
    ask_smem.start()

    def use_copy(k, chunk):
        return remote(
            picked.at[k - 1, chunk], used.at[Y - k - 1, chunk],
            ys.at[k - 1], yr.at[Y - k - 1], in_rows(turn(y, k, Y), z),
        )

    def send_uses(chunk):
        hold[...] = zbuf[pl.ds(chunk * 8, 8)]
        for k in (2, 1, 3):
            for rank in range(2):
                picked[k - 1, chunk, rank] = hold[asked_s[k - 1, chunk, rank]]
            use_copy(k, chunk).start()

    def forward(step, pieces):
        for piece in pieces:
            for way in range(2):
                arriving(way, step - 1, piece).wait_recv()
                sent(way, step, piece).start()

    forward(1, range(SUB // 2))
    ask_smem.wait()
    send_uses(z)
    forward(1, range(SUB // 2, SUB))
    for way in range(2):
        send_uses(turn(z, -1 if way == 0 else 1, Z))

    def ring_step(step, carry):
        forward(step, range(SUB))
        for way in range(2):
            send_uses(turn(z, -step if way == 0 else step, Z))
        return carry

    lax.fori_loop(2, HALF - 1, ring_step, 0)
    for piece in range(SUB):
        for way in range(2):
            arriving(way, HALF - 2, piece).wait_recv()
            if way == last_way(piece):
                sent(way, HALF - 1, piece).start()
    for way in range(2):
        send_uses(turn(z, 1 - HALF if way == 0 else HALF - 1, Z))
    for piece in range(SUB):
        arriving(last_way(piece), HALF - 1, piece).wait_recv()
    send_uses(turn(z, HALF, Z))

    def ring_end():
        for way in range(2):
            all_sent = zbuf.at[pl.ds(0, 8 * HALF - 4)]
            remote(all_sent, all_sent, zs.at[way], zr.at[way, 0, 0], right).wait_send()

    ends.append(ring_end)

    def all_uses(k):
        return remote(
            picked.at[k - 1], used.at[Y - k - 1], ys.at[k - 1], yr.at[Y - k - 1],
            in_rows(turn(y, k, Y), z),
        )

    def uses_left():
        for k in range(1, Y):
            all_uses(k).wait_send()

    ends.append(uses_left)
    later[1].wait()
    ones = jnp.ones((8, 128), BF)
    for b in range(8):
        total = dot(ones, adj[b, 0], 1, 1) + dot(ones, adj[b, 1], 1, 1)
        scale[b] = 1.0 / jnp.sqrt(1.0 + total)
    for c in to_smem:
        c.wait()
    all_f.wait_recv()
    later[2].wait()
    pre_self[...] = dot(own_f[...], ws[...], 0, 0)
    for k in range(1, Y):
        all_uses(k).wait_recv()
    def use(k, b):
        block = nb_s[k, b]
        owner = block // 8
        ahead = lax.rem(owner // Z - y + Y, Y)
        rank = jnp.where(table_s[owner, 2] == 8 * k + b, 0, 1)
        other = used[jnp.maximum(ahead, 1) - 1, lax.rem(owner, Z), rank]
        return jnp.where(ahead == 0, zbuf[lax.rem(block, 8 * Z)], other)

    def agg_copy(k, q, source):
        return remote(
            lhs.at[mine_a, pl.ds(pl.multiple_of(q * 128, 128), 128)],
            own_a.at[pl.ds(pl.multiple_of(source * 64, 64), 64)],
            as_.at[0], ar.at[0], in_rep(q),
        )

    for k in (4, 3, 5, 2, 6, 1, 7, 0):
        b = turn(rep, k, REP)
        raw = dot(use(0, b), adj[b, 0], 1, 1) + dot(use(1, b), adj[b, 1], 1, 1)
        agg = (raw * scale[b, 0:1, :]).astype(BF)
        lhs[mine_a, pl.ds(pl.multiple_of(128 * b, 128), 128)] = agg
        if k:
            agg_copy(k, b, rep).start()
        else:
            own_a[own_rows] = agg
    some_a = own_a.at[pl.ds(0, 448)]
    all_a = remote(some_a, some_a, as_.at[0], ar.at[0], in_rep(turn(rep, 1, REP)))
    pair_a = remote(lhs.at[mine_a], lhs.at[mine_a], ps.at[1], pr.at[1], pair)
    go(pair_a)
    finish()
    later[3].wait()
    later[4].wait()
    all_a.wait_recv()
    ends.append(all_a.wait_send)


    def g_copy(k, q, source):
        return remote(
            g_own.at[:, pl.ds(256 * (k % 2), 256)],
            g_all.at[pl.ds(pl.multiple_of(source * 128, 128), 128)],
            gs.at[0], gr.at[0], in_rep(q),
        )

    for half in range(2):
        cols = slice(256 * half, 256 * half + 256)
        pre = pre_self[:, cols] + dot(own_a[...], wn[:, cols], 0, 0)
        s = 1.0 / (1.0 + jnp.exp(-pre))
        g_own[:, cols] = (cot[:, cols].astype(F32) * (s * (1.0 + pre * (1.0 - s)))).astype(BF)
        out_ref[:, cols] = (pre * s).astype(BF)
        for step in (2, 1, 3):
            chip = turn(x, step, X)
            g_copy(2 * step + half, 2 * chip + half, rep).start()

        @pl.when(core != half)
        def _():
            g_copy(half, 2 * x + half, rep).start()

    some_g = g_all.at[pl.ds(0, 896)]
    all_g = remote(some_g, some_g, gs.at[0], gr.at[0], in_rep(turn(rep, 1, REP)))
    g_all[pl.ds(pl.multiple_of(rep * 128, 128), 128)] = g_own[
        :, pl.ds(pl.multiple_of(core * 256, 256), 256)
    ]
    finish()
    other = pl.ds(pl.multiple_of(64 - core * 64, 64), 64)
    other_a = pl.ds(pl.multiple_of(192 - core * 64, 64), 64)
    remote(lhs.at[other], lhs.at[other], ps.at[0], pr.at[0], pair).wait_recv()
    remote(lhs.at[other_a], lhs.at[other_a], ps.at[1], pr.at[1], pair).wait_recv()
    all_g.wait_recv()
    ends.append(all_g.wait_send)
    grad = dot(lhs[...], g_all[...], 1, 0)
    for q in range(4):
        cols = slice(64 * q, 64 * q + 64)
        part = jnp.concatenate([grad[:128, cols], grad[128:, cols]], axis=1)
        parts[q] = part.astype(BF)

    def part_copy(q, source):
        return remote(
            parts.at[q], y_in.at[source], ts.at[q], tr.at[source],
            {"rows": x * Z + z, "rep": 4 * core + q},
        )

    def part_stays(q):
        return jnp.logical_and(x == y, 4 * core + q == rep)

    for q in range(4):
        keep = pltpu.make_async_copy(parts.at[q], y_in.at[y], tr.at[y])
        stays = part_stays(q)
        pl.when(stays)(keep.start)
        pl.when(jnp.logical_not(stays))(part_copy(q, y).start)
    total = jnp.zeros((128, 128), F32)
    for source in range(4):
        part_copy(0, source).wait_recv()
        total = total + y_in[source].astype(F32)
    y_sum[...] = total.reshape(Z, 8, 128)

    def last_copy(j, source):
        a = turn(z, j, Z)
        return remote(
            y_sum.at[a], z_in.at[source], us.at[0], ur.at[0], in_rows(y, a)
        )

    for j in (8, 7, 9, 6, 10, 5, 11, 4, 12, 3, 13, 2, 14, 1, 15):
        last_copy(j, z).start()
    z_in[z] = y_sum[z]
    finish()
    for q in range(4):
        pl.when(jnp.logical_not(part_stays(q)))(part_copy(q, y).wait_send)
    some_z = z_in.at[pl.ds(0, Z - 1)]
    all_z = remote(some_z, some_z, us.at[0], ur.at[0], right)
    all_z.wait_recv()
    grads = z_in[0]
    for a in range(1, Z):
        grads = grads + z_in[a]
    wg_ref[0] = grads[:, :64]
    wg_ref[1] = grads[:, 64:]
    all_z.wait_send()


def local(features, neighbor_blocks, adjacency, w_self, w_neigh, cotangent):
    vmem, anywhere = pl.BlockSpec(memory_space=pltpu.VMEM), pl.BlockSpec(memory_space=pl.ANY)
    dma = pltpu.SemaphoreType.DMA
    return pl.pallas_call(
        kernel,
        out_shape=(
            jax.ShapeDtypeStruct((128, 512), BF),
            jax.ShapeDtypeStruct((2, 8, 64), F32),
        ),
        in_specs=[anywhere] * 6,
        out_specs=(vmem, vmem),
        scratch_shapes=[
            pltpu.VMEM((128, 64, 128), BF),
            pltpu.VMEM((8, 64, 128), BF),
            pltpu.VMEM((3, 16, 2, 64, 128), BF),
            pltpu.VMEM((3, 16, 2, 64, 128), BF),
            pltpu.VMEM((512, 128), BF),
            pltpu.VMEM((512, 128), BF),
            pltpu.VMEM((256, 1024), BF),
            pltpu.VMEM((8, 2, 128, 128), BF),
            pltpu.VMEM((512, 512), BF),
            pltpu.VMEM((512, 512), BF),
            pltpu.VMEM((128, 512), BF),
            pltpu.VMEM((8, 8, 128), F32),
            pltpu.VMEM((128, 512), F32),
            pltpu.VMEM((128, 512), BF),
            pltpu.VMEM((1024, 256), BF),
            pltpu.VMEM((4, 128, 128), BF),
            pltpu.VMEM((4, 128, 128), BF),
            pltpu.VMEM((16, 8, 128), F32),
            pltpu.VMEM((16, 8, 128), F32),
            pltpu.VMEM((64, 128), jnp.int32),
            pltpu.VMEM((3, 16, 128), jnp.int32),
            pltpu.VMEM((2, 8), jnp.int32),
            pltpu.SMEM((2, 8), jnp.int32),
            pltpu.SMEM((64, 128), jnp.int32),
            pltpu.SMEM((3, 16, 128), jnp.int32),
            dma((17,)),
            dma((2,)), dma((2, HALF, SUB)),
            dma((1,)), dma((1,)),
            dma((1,)), dma((1,)),
            dma((1,)), dma((1,)),
            dma((2,)), dma((2,)),
            dma((3,)), dma((3,)),
            dma((3,)), dma((3,)),
            dma((4,)), dma((4,)),
            dma((1,)), dma((1,)),
        ],
        compiler_params=pltpu.CompilerParams(
            collective_id=0, has_side_effects=True, vmem_limit_bytes=60 * 1024 * 1024
        ),
        cost_estimate=pl.CostEstimate(
            flops=500_000_000, bytes_accessed=2_500_000, transcendentals=65536
        ),
    )(neighbor_blocks.T, features.T, adjacency, w_self, w_neigh, cotangent)


def solution(mesh):
    in_specs = (
        P("rows", "rep"),
        P("rows", None),
        P("rows", None, None, None),
        P(),
        P(),
        P(("rows", "rep"), None),
    )
    out_specs = (P(("rows", "rep"), None), P(None, "rows", "rep"))
    return jax.shard_map(local, mesh=mesh, in_specs=in_specs, out_specs=out_specs, check_vma=False)
```

```python
import jax
import jax.numpy as jnp
from jax import lax
from jax.experimental import pallas as pl
from jax.experimental.pallas import tpu as pltpu
from jax.sharding import PartitionSpec as P

Y, Z, X = 4, 16, 4
REP = 2 * X
SUB = 4
PIECE = 8 // SUB
HALF = Z // 2
MESH = pl.DeviceIdType.MESH
BF, F32 = jnp.bfloat16, jnp.float32


def dot(a, b, ca, cb):
    return lax.dot_general(a, b, (((ca,), (cb,)), ((), ())), preferred_element_type=F32)


def kernel(
    nb_hbm, f_hbm, adj_hbm, ws_hbm, wn_hbm, cot_hbm,
    out_ref, wg_ref,
    zbuf, hold, picked, used, own_f, own_a, lhs, adj, ws, wn, cot,
    scale, pre_self, g_own, g_all, parts, y_in, y_sum, z_in, table, asked, nb_v, nb_s, table_s, asked_s,
    load_sem, zs, zr, fs, fr, as_, ar, gs, gr, ps, pr, ns, nr, ys, yr, ts, tr, us, ur,
):
    row, rep = lax.axis_index("rows"), lax.axis_index("rep")
    y, z = row // Z, lax.rem(row, Z)
    x, core = rep // 2, lax.rem(rep, 2)

    def in_rows(yy, zz):
        return {"rows": yy * Z + zz, "rep": rep}

    def in_rep(q):
        return {"rows": row, "rep": q}

    def remote(src, dst, send, recv, device):
        return pltpu.make_async_remote_copy(
            src_ref=src, dst_ref=dst, send_sem=send, recv_sem=recv,
            device_id=device, device_id_type=MESH,
        )

    def turn(a, k, n):
        return lax.rem(a + k + n, n)

    right, left = in_rows(y, turn(z, 1, Z)), in_rows(y, turn(z, -1, Z))

    ends = []

    def go(copy):
        copy.start()
        ends.append(copy.wait_send)

    def finish():
        for end in ends:
            end()
        ends.clear()

    first = [
        pltpu.make_async_copy(
            f_hbm.at[:, pl.ds(128 * l, 128)], zbuf.at[z * 8 + l], load_sem.at[l]
        )
        for l in range(8)
    ]
    mine = pl.ds(pl.multiple_of(core * 64, 64), 64)
    mine_a = pl.ds(pl.multiple_of(128 + core * 64, 64), 64)
    later = [
        pltpu.make_async_copy(f_hbm, lhs.at[mine], load_sem.at[8]),
        pltpu.make_async_copy(adj_hbm, adj, load_sem.at[9]),
        pltpu.make_async_copy(ws_hbm, ws, load_sem.at[10]),
        pltpu.make_async_copy(wn_hbm, wn, load_sem.at[11]),
        pltpu.make_async_copy(cot_hbm, cot, load_sem.at[12]),
    ]
    numbers = pltpu.make_async_copy(nb_hbm, nb_v, load_sem.at[16])
    numbers.start()
    for c in first:
        c.start()

    barrier = pltpu.get_barrier_semaphore()
    for device in (right, left):
        pl.semaphore_signal(barrier, inc=1, device_id=device, device_id_type=MESH)
    for k in range(1, Y):
        pl.semaphore_signal(
            barrier, inc=1, device_id=in_rows(turn(y, k, Y), z), device_id_type=MESH
        )
    for k in range(1, REP):
        pl.semaphore_signal(
            barrier, inc=1, device_id=in_rep(turn(rep, k, REP)), device_id_type=MESH
        )
    for c in later:
        c.start()
    numbers.wait()
    owner_id = lax.broadcasted_iota(jnp.int32, (64, 8), 0)
    lane = lax.broadcasted_iota(jnp.int32, (64, 8), 1)
    low = jnp.full((64, 1), 255, jnp.int32)
    high = jnp.zeros((64, 1), jnp.int32)
    for k in range(2):
        block = nb_v[k : k + 1, :]
        named = block // 8 == owner_id
        code = (8 * k + lane) * 8 + block % 8
        low = jnp.minimum(low, jnp.min(jnp.where(named, code, 255), axis=1, keepdims=True))
        high = jnp.maximum(high, jnp.max(jnp.where(named, code, 0), axis=1, keepdims=True))
    lane = lax.broadcasted_iota(jnp.int32, (64, 128), 1)
    table[...] = jnp.where(lane == 0, low % 8, jnp.where(lane == 1, high % 8, low // 8))
    to_smem = [
        pltpu.make_async_copy(nb_v, nb_s, load_sem.at[13]),
        pltpu.make_async_copy(table, table_s, load_sem.at[14]),
    ]
    for c in to_smem:
        c.start()
    for c in first:
        c.wait()
    pl.semaphore_wait(barrier, 2 + (Y - 1) + (REP - 1))

    def table_copy(k):
        yy = turn(y, k, Y)
        return remote(
            table.at[pl.ds(yy * Z, Z)], asked.at[Y - k - 1], ns.at[k - 1], nr.at[k - 1],
            in_rows(yy, z),
        )


    def ring_copy(way, step, piece, chunk):
        at = pl.ds(chunk * 8 + piece * PIECE, PIECE)
        return remote(
            zbuf.at[at], zbuf.at[at], zs.at[way], zr.at[way, step, piece],
            right if way == 0 else left,
        )

    def sent(way, step, piece):
        return ring_copy(way, step, piece, turn(z, -step if way == 0 else step, Z))

    def arriving(way, step, piece):
        return ring_copy(way, step, piece, turn(z, -1 - step if way == 0 else 1 + step, Z))

    def last_way(piece):
        return 0 if piece < SUB // 2 else 1

    for way in range(2):
        sent(way, 0, 0).start()
    for k in (2, 1, 3):
        go(table_copy(k))
    for piece in range(1, SUB):
        for way in range(2):
            sent(way, 0, piece).start()

    def feature_copy(k, q, source):
        return remote(
            zbuf.at[z * 8 + q], own_f.at[pl.ds(pl.multiple_of(source * 64, 64), 64)],
            fs.at[0], fr.at[0], in_rep(q),
        )

    for k in range(1, REP):
        feature_copy(k, turn(rep, k, REP), rep).start()
    some_f = own_f.at[pl.ds(0, 448)]
    all_f = remote(some_f, some_f, fs.at[0], fr.at[0], in_rep(turn(rep, 1, REP)))
    ends.append(all_f.wait_send)
    later[0].wait()
    pair = in_rep(x * 2 + 1 - core)
    pair_f = remote(lhs.at[mine], lhs.at[mine], ps.at[0], pr.at[0], pair)
    go(pair_f)
    own_rows = pl.ds(pl.multiple_of(rep * 64, 64), 64)
    own_f[own_rows] = zbuf[z * 8 + rep]

    for k in range(1, Y):
        table_copy(k).wait_recv()
    ask_smem = pltpu.make_async_copy(asked, asked_s, load_sem.at[15])
    ask_smem.start()

    def use_copy(k, chunk):
        return remote(
            picked.at[k - 1, chunk], used.at[Y - k - 1, chunk],
            ys.at[k - 1], yr.at[Y - k - 1], in_rows(turn(y, k, Y), z),
        )

    def send_uses(chunk):
        hold[...] = zbuf[pl.ds(chunk * 8, 8)]
        for k in (2, 1, 3):
            for rank in range(2):
                picked[k - 1, chunk, rank] = hold[asked_s[k - 1, chunk, rank]]
            use_copy(k, chunk).start()

    def forward(step, pieces):
        for piece in pieces:
            for way in range(2):
                arriving(way, step - 1, piece).wait_recv()
                sent(way, step, piece).start()

    forward(1, range(SUB // 2))
    ask_smem.wait()
    send_uses(z)
    forward(1, range(SUB // 2, SUB))
    for way in range(2):
        send_uses(turn(z, -1 if way == 0 else 1, Z))

    def ring_step(step, carry):
        forward(step, range(SUB))
        for way in range(2):
            send_uses(turn(z, -step if way == 0 else step, Z))
        return carry

    lax.fori_loop(2, HALF - 1, ring_step, 0)
    for piece in range(SUB):
        for way in range(2):
            arriving(way, HALF - 2, piece).wait_recv()
            if way == last_way(piece):
                sent(way, HALF - 1, piece).start()
    for way in range(2):
        send_uses(turn(z, 1 - HALF if way == 0 else HALF - 1, Z))
    for piece in range(SUB):
        arriving(last_way(piece), HALF - 1, piece).wait_recv()
    send_uses(turn(z, HALF, Z))

    def ring_end():
        for way in range(2):
            all_sent = zbuf.at[pl.ds(0, 8 * HALF - 4)]
            remote(all_sent, all_sent, zs.at[way], zr.at[way, 0, 0], right).wait_send()

    ends.append(ring_end)

    def all_uses(k):
        return remote(
            picked.at[k - 1], used.at[Y - k - 1], ys.at[k - 1], yr.at[Y - k - 1],
            in_rows(turn(y, k, Y), z),
        )

    def uses_left():
        for k in range(1, Y):
            all_uses(k).wait_send()

    ends.append(uses_left)
    later[1].wait()
    ones = jnp.ones((8, 128), BF)
    for b in range(8):
        total = dot(ones, adj[b, 0], 1, 1) + dot(ones, adj[b, 1], 1, 1)
        scale[b] = 1.0 / jnp.sqrt(1.0 + total)
    for c in to_smem:
        c.wait()
    all_f.wait_recv()
    later[2].wait()
    pre_self[...] = dot(own_f[...], ws[...], 0, 0)
    for k in range(1, Y):
        all_uses(k).wait_recv()
    def use(k, b):
        block = nb_s[k, b]
        owner = block // 8
        ahead = lax.rem(owner // Z - y + Y, Y)
        rank = jnp.where(table_s[owner, 2] == 8 * k + b, 0, 1)
        other = used[jnp.maximum(ahead, 1) - 1, lax.rem(owner, Z), rank]
        return jnp.where(ahead == 0, zbuf[lax.rem(block, 8 * Z)], other)

    def agg_copy(k, q, source):
        return remote(
            lhs.at[mine_a, pl.ds(pl.multiple_of(q * 128, 128), 128)],
            own_a.at[pl.ds(pl.multiple_of(source * 64, 64), 64)],
            as_.at[0], ar.at[0], in_rep(q),
        )

    for k in (4, 3, 5, 2, 6, 1, 7, 0):
        b = turn(rep, k, REP)
        raw = dot(use(0, b), adj[b, 0], 1, 1) + dot(use(1, b), adj[b, 1], 1, 1)
        agg = (raw * scale[b, 0:1, :]).astype(BF)
        lhs[mine_a, pl.ds(pl.multiple_of(128 * b, 128), 128)] = agg
        if k:
            agg_copy(k, b, rep).start()
        else:
            own_a[own_rows] = agg
    some_a = own_a.at[pl.ds(0, 448)]
    all_a = remote(some_a, some_a, as_.at[0], ar.at[0], in_rep(turn(rep, 1, REP)))
    pair_a = remote(lhs.at[mine_a], lhs.at[mine_a], ps.at[1], pr.at[1], pair)
    go(pair_a)
    finish()
    later[3].wait()
    later[4].wait()
    all_a.wait_recv()
    ends.append(all_a.wait_send)


    def g_copy(k, q, source):
        return remote(
            g_own.at[:, pl.ds(256 * (k % 2), 256)],
            g_all.at[pl.ds(pl.multiple_of(source * 128, 128), 128)],
            gs.at[0], gr.at[0], in_rep(q),
        )

    for half in range(2):
        cols = slice(256 * half, 256 * half + 256)
        pre = pre_self[:, cols] + dot(own_a[...], wn[:, cols], 0, 0)
        s = jax.nn.sigmoid(pre)
        g_own[:, cols] = (cot[:, cols].astype(F32) * (s * (1.0 + pre * (1.0 - s)))).astype(BF)
        out_ref[:, cols] = (pre * s).astype(BF)
        for step in (2, 1, 3):
            chip = turn(x, step, X)
            g_copy(2 * step + half, 2 * chip + half, rep).start()

        @pl.when(core != half)
        def _():
            g_copy(half, 2 * x + half, rep).start()

    some_g = g_all.at[pl.ds(0, 896)]
    all_g = remote(some_g, some_g, gs.at[0], gr.at[0], in_rep(turn(rep, 1, REP)))
    g_all[pl.ds(pl.multiple_of(rep * 128, 128), 128)] = g_own[
        :, pl.ds(pl.multiple_of(core * 256, 256), 256)
    ]
    finish()
    other = pl.ds(pl.multiple_of(64 - core * 64, 64), 64)
    other_a = pl.ds(pl.multiple_of(192 - core * 64, 64), 64)
    remote(lhs.at[other], lhs.at[other], ps.at[0], pr.at[0], pair).wait_recv()
    remote(lhs.at[other_a], lhs.at[other_a], ps.at[1], pr.at[1], pair).wait_recv()
    all_g.wait_recv()
    ends.append(all_g.wait_send)
    grad = dot(lhs[...], g_all[...], 1, 0)
    for q in range(4):
        cols = slice(64 * q, 64 * q + 64)
        part = jnp.concatenate([grad[:128, cols], grad[128:, cols]], axis=1)
        parts[q] = part.astype(BF)

    def part_copy(q, source):
        return remote(
            parts.at[q], y_in.at[source], ts.at[q], tr.at[source],
            {"rows": x * Z + z, "rep": 4 * core + q},
        )

    def part_stays(q):
        return jnp.logical_and(x == y, 4 * core + q == rep)

    for q in range(4):
        keep = pltpu.make_async_copy(parts.at[q], y_in.at[y], tr.at[y])
        stays = part_stays(q)
        pl.when(stays)(keep.start)
        pl.when(jnp.logical_not(stays))(part_copy(q, y).start)
    total = jnp.zeros((128, 128), F32)
    for source in range(4):
        part_copy(0, source).wait_recv()
        total = total + y_in[source].astype(F32)
    y_sum[...] = total.reshape(Z, 8, 128)

    def last_copy(j, source):
        a = turn(z, j, Z)
        return remote(
            y_sum.at[a], z_in.at[source], us.at[0], ur.at[0], in_rows(y, a)
        )

    for j in (8, 7, 9, 6, 10, 5, 11, 4, 12, 3, 13, 2, 14, 1, 15):
        last_copy(j, z).start()
    z_in[z] = y_sum[z]
    finish()
    for q in range(4):
        pl.when(jnp.logical_not(part_stays(q)))(part_copy(q, y).wait_send)
    some_z = z_in.at[pl.ds(0, Z - 1)]
    all_z = remote(some_z, some_z, us.at[0], ur.at[0], right)
    all_z.wait_recv()
    grads = z_in[0]
    for a in range(1, Z):
        grads = grads + z_in[a]
    wg_ref[0] = grads[:, :64]
    wg_ref[1] = grads[:, 64:]
    all_z.wait_send()


def local(features, neighbor_blocks, adjacency, w_self, w_neigh, cotangent):
    vmem, anywhere = pl.BlockSpec(memory_space=pltpu.VMEM), pl.BlockSpec(memory_space=pl.ANY)
    dma = pltpu.SemaphoreType.DMA
    return pl.pallas_call(
        kernel,
        out_shape=(
            jax.ShapeDtypeStruct((128, 512), BF),
            jax.ShapeDtypeStruct((2, 8, 64), F32),
        ),
        in_specs=[anywhere] * 6,
        out_specs=(vmem, vmem),
        scratch_shapes=[
            pltpu.VMEM((128, 64, 128), BF),
            pltpu.VMEM((8, 64, 128), BF),
            pltpu.VMEM((3, 16, 2, 64, 128), BF),
            pltpu.VMEM((3, 16, 2, 64, 128), BF),
            pltpu.VMEM((512, 128), BF),
            pltpu.VMEM((512, 128), BF),
            pltpu.VMEM((256, 1024), BF),
            pltpu.VMEM((8, 2, 128, 128), BF),
            pltpu.VMEM((512, 512), BF),
            pltpu.VMEM((512, 512), BF),
            pltpu.VMEM((128, 512), BF),
            pltpu.VMEM((8, 8, 128), F32),
            pltpu.VMEM((128, 512), F32),
            pltpu.VMEM((128, 512), BF),
            pltpu.VMEM((1024, 256), BF),
            pltpu.VMEM((4, 128, 128), BF),
            pltpu.VMEM((4, 128, 128), BF),
            pltpu.VMEM((16, 8, 128), F32),
            pltpu.VMEM((16, 8, 128), F32),
            pltpu.VMEM((64, 128), jnp.int32),
            pltpu.VMEM((3, 16, 128), jnp.int32),
            pltpu.VMEM((2, 8), jnp.int32),
            pltpu.SMEM((2, 8), jnp.int32),
            pltpu.SMEM((64, 128), jnp.int32),
            pltpu.SMEM((3, 16, 128), jnp.int32),
            dma((17,)),
            dma((2,)), dma((2, HALF, SUB)),
            dma((1,)), dma((1,)),
            dma((1,)), dma((1,)),
            dma((1,)), dma((1,)),
            dma((2,)), dma((2,)),
            dma((3,)), dma((3,)),
            dma((3,)), dma((3,)),
            dma((4,)), dma((4,)),
            dma((1,)), dma((1,)),
        ],
        compiler_params=pltpu.CompilerParams(
            collective_id=0, has_side_effects=True, vmem_limit_bytes=60 * 1024 * 1024
        ),
        cost_estimate=pl.CostEstimate(
            flops=500_000_000, bytes_accessed=2_500_000, transcendentals=65536
        ),
    )(neighbor_blocks.T, features.T, adjacency, w_self, w_neigh, cotangent)


def solution(mesh):
    in_specs = (
        P("rows", "rep"),
        P("rows", None),
        P("rows", None, None, None),
        P(),
        P(),
        P(("rows", "rep"), None),
    )
    out_specs = (P(("rows", "rep"), None), P(None, "rows", "rep"))
    return jax.shard_map(local, mesh=mesh, in_specs=in_specs, out_specs=out_specs, check_vma=False)
```

```python
import jax
import jax.numpy as jnp
from jax import lax
from jax.experimental import pallas as pl
from jax.experimental.pallas import tpu as pltpu
from jax.sharding import PartitionSpec as P

Y, Z, X = 4, 16, 4
REP = 2 * X
SUB = 4
PIECE = 8 // SUB
HALF = Z // 2
MESH = pl.DeviceIdType.MESH
BF, F32 = jnp.bfloat16, jnp.float32


def dot(a, b, ca, cb):
    return lax.dot_general(a, b, (((ca,), (cb,)), ((), ())), preferred_element_type=F32)


def kernel(
    nb_hbm, f_hbm, adj_hbm, ws_hbm, wn_hbm, cot_hbm,
    out_ref, wg_ref,
    zbuf, hold, picked, used, own_f, own_a, lhs, adj, ws, wn, cot,
    scale, pre_self, g_own, g_all, parts, y_in, y_sum, z_in, table, asked, nb_v, nb_s, table_s, asked_s,
    load_sem, zs, zr, fs, fr, as_, ar, gs, gr, ps, pr, ns, nr, ys, yr, ts, tr, us, ur,
):
    row, rep = lax.axis_index("rows"), lax.axis_index("rep")
    y, z = row // Z, lax.rem(row, Z)
    x, core = rep // 2, lax.rem(rep, 2)

    def in_rows(yy, zz):
        return {"rows": yy * Z + zz, "rep": rep}

    def in_rep(q):
        return {"rows": row, "rep": q}

    def remote(src, dst, send, recv, device):
        return pltpu.make_async_remote_copy(
            src_ref=src, dst_ref=dst, send_sem=send, recv_sem=recv,
            device_id=device, device_id_type=MESH,
        )

    def turn(a, k, n):
        return lax.rem(a + k + n, n)

    right, left = in_rows(y, turn(z, 1, Z)), in_rows(y, turn(z, -1, Z))

    ends = []

    def go(copy):
        copy.start()
        ends.append(copy.wait_send)

    def finish():
        for end in ends:
            end()
        ends.clear()

    first = [
        pltpu.make_async_copy(
            f_hbm.at[:, pl.ds(128 * l, 128)], zbuf.at[z * 8 + l], load_sem.at[l]
        )
        for l in range(8)
    ]
    mine = pl.ds(pl.multiple_of(core * 64, 64), 64)
    mine_a = pl.ds(pl.multiple_of(128 + core * 64, 64), 64)
    later = [
        pltpu.make_async_copy(f_hbm, lhs.at[mine], load_sem.at[8]),
        pltpu.make_async_copy(adj_hbm, adj, load_sem.at[9]),
        pltpu.make_async_copy(ws_hbm, ws, load_sem.at[10]),
        pltpu.make_async_copy(wn_hbm, wn, load_sem.at[11]),
        pltpu.make_async_copy(cot_hbm, cot, load_sem.at[12]),
    ]
    numbers = pltpu.make_async_copy(nb_hbm, nb_v, load_sem.at[16])
    numbers.start()
    for c in first:
        c.start()

    barrier = pltpu.get_barrier_semaphore()
    for device in (right, left):
        pl.semaphore_signal(barrier, inc=1, device_id=device, device_id_type=MESH)
    for k in range(1, Y):
        pl.semaphore_signal(
            barrier, inc=1, device_id=in_rows(turn(y, k, Y), z), device_id_type=MESH
        )
    for k in range(1, REP):
        pl.semaphore_signal(
            barrier, inc=1, device_id=in_rep(turn(rep, k, REP)), device_id_type=MESH
        )
    for c in later:
        c.start()
    numbers.wait()
    owner_id = lax.broadcasted_iota(jnp.int32, (64, 8), 0)
    lane = lax.broadcasted_iota(jnp.int32, (64, 8), 1)
    low = jnp.full((64, 1), 255, jnp.int32)
    high = jnp.zeros((64, 1), jnp.int32)
    for k in range(2):
        block = nb_v[k : k + 1, :]
        named = block // 8 == owner_id
        code = (8 * k + lane) * 8 + block % 8
        low = jnp.minimum(low, jnp.min(jnp.where(named, code, 255), axis=1, keepdims=True))
        high = jnp.maximum(high, jnp.max(jnp.where(named, code, 0), axis=1, keepdims=True))
    lane = lax.broadcasted_iota(jnp.int32, (64, 128), 1)
    table[...] = jnp.where(lane == 0, low % 8, jnp.where(lane == 1, high % 8, low // 8))
    to_smem = [
        pltpu.make_async_copy(nb_v, nb_s, load_sem.at[13]),
        pltpu.make_async_copy(table, table_s, load_sem.at[14]),
    ]
    for c in to_smem:
        c.start()
    for c in first:
        c.wait()
    pl.semaphore_wait(barrier, 2 + (Y - 1) + (REP - 1))

    def table_copy(k):
        yy = turn(y, k, Y)
        return remote(
            table.at[pl.ds(yy * Z, Z)], asked.at[Y - k - 1], ns.at[k - 1], nr.at[k - 1],
            in_rows(yy, z),
        )


    def ring_copy(way, step, piece, chunk):
        at = pl.ds(chunk * 8 + piece * PIECE, PIECE)
        return remote(
            zbuf.at[at], zbuf.at[at], zs.at[way], zr.at[way, step, piece],
            right if way == 0 else left,
        )

    def sent(way, step, piece):
        return ring_copy(way, step, piece, turn(z, -step if way == 0 else step, Z))

    def arriving(way, step, piece):
        return ring_copy(way, step, piece, turn(z, -1 - step if way == 0 else 1 + step, Z))

    def last_way(piece):
        return 0 if piece < SUB // 2 else 1

    for way in range(2):
        sent(way, 0, 0).start()
    for k in (2, 1, 3):
        go(table_copy(k))
    for piece in range(1, SUB):
        for way in range(2):
            sent(way, 0, piece).start()

    def feature_copy(k, q, source):
        return remote(
            zbuf.at[z * 8 + q], own_f.at[pl.ds(pl.multiple_of(source * 64, 64), 64)],
            fs.at[0], fr.at[0], in_rep(q),
        )

    for k in range(1, REP):
        feature_copy(k, turn(rep, k, REP), rep).start()
    some_f = own_f.at[pl.ds(0, 448)]
    all_f = remote(some_f, some_f, fs.at[0], fr.at[0], in_rep(turn(rep, 1, REP)))
    ends.append(all_f.wait_send)
    later[0].wait()
    pair = in_rep(x * 2 + 1 - core)
    pair_f = remote(lhs.at[mine], lhs.at[mine], ps.at[0], pr.at[0], pair)
    go(pair_f)
    own_rows = pl.ds(pl.multiple_of(rep * 64, 64), 64)
    own_f[own_rows] = zbuf[z * 8 + rep]

    for k in range(1, Y):
        table_copy(k).wait_recv()
    ask_smem = pltpu.make_async_copy(asked, asked_s, load_sem.at[15])
    ask_smem.start()

    def use_copy(k, chunk):
        return remote(
            picked.at[k - 1, chunk], used.at[Y - k - 1, chunk],
            ys.at[k - 1], yr.at[Y - k - 1], in_rows(turn(y, k, Y), z),
        )

    def send_uses(chunk):
        hold[...] = zbuf[pl.ds(chunk * 8, 8)]
        for k in (2, 1, 3):
            for rank in range(2):
                picked[k - 1, chunk, rank] = hold[asked_s[k - 1, chunk, rank]]
            use_copy(k, chunk).start()

    def forward(step, pieces):
        for piece in pieces:
            for way in range(2):
                arriving(way, step - 1, piece).wait_recv()
                sent(way, step, piece).start()

    forward(1, range(SUB // 2))
    ask_smem.wait()
    send_uses(z)
    forward(1, range(SUB // 2, SUB))
    for way in range(2):
        send_uses(turn(z, -1 if way == 0 else 1, Z))

    def ring_step(step, carry):
        forward(step, range(SUB))
        for way in range(2):
            send_uses(turn(z, -step if way == 0 else step, Z))
        return carry

    lax.fori_loop(2, HALF - 1, ring_step, 0)
    for piece in range(SUB):
        for way in range(2):
            arriving(way, HALF - 2, piece).wait_recv()
            if way == last_way(piece):
                sent(way, HALF - 1, piece).start()
    for way in range(2):
        send_uses(turn(z, 1 - HALF if way == 0 else HALF - 1, Z))
    for piece in range(SUB):
        arriving(last_way(piece), HALF - 1, piece).wait_recv()
    send_uses(turn(z, HALF, Z))

    def ring_end():
        for way in range(2):
            all_sent = zbuf.at[pl.ds(0, 8 * HALF - 4)]
            remote(all_sent, all_sent, zs.at[way], zr.at[way, 0, 0], right).wait_send()

    ends.append(ring_end)

    def all_uses(k):
        return remote(
            picked.at[k - 1], used.at[Y - k - 1], ys.at[k - 1], yr.at[Y - k - 1],
            in_rows(turn(y, k, Y), z),
        )

    def uses_left():
        for k in range(1, Y):
            all_uses(k).wait_send()

    ends.append(uses_left)
    later[1].wait()
    ones = jnp.ones((8, 128), BF)
    for b in range(8):
        total = dot(ones, adj[b, 0], 1, 1) + dot(ones, adj[b, 1], 1, 1)
        scale[b] = 1.0 / jnp.sqrt(1.0 + total)
    for c in to_smem:
        c.wait()
    all_f.wait_recv()
    later[2].wait()
    pre_self[...] = dot(own_f[...], ws[...], 0, 0)
    for k in range(1, Y):
        all_uses(k).wait_recv()
    def use(k, b):
        block = nb_s[k, b]
        owner = block // 8
        ahead = lax.rem(owner // Z - y + Y, Y)
        rank = jnp.where(table_s[owner, 2] == 8 * k + b, 0, 1)
        other = used[jnp.maximum(ahead, 1) - 1, lax.rem(owner, Z), rank]
        return jnp.where(ahead == 0, zbuf[lax.rem(block, 8 * Z)], other)

    def agg_copy(k, q, source):
        return remote(
            lhs.at[mine_a, pl.ds(pl.multiple_of(q * 128, 128), 128)],
            own_a.at[pl.ds(pl.multiple_of(source * 64, 64), 64)],
            as_.at[0], ar.at[0], in_rep(q),
        )

    for k in (4, 3, 5, 2, 6, 1, 7, 0):
        b = turn(rep, k, REP)
        both = jnp.concatenate([use(0, b), use(1, b)], axis=1)
        raw = dot(both, jnp.concatenate([adj[b, 0], adj[b, 1]], axis=1), 1, 1)
        agg = (raw * scale[b, 0:1, :]).astype(BF)
        lhs[mine_a, pl.ds(pl.multiple_of(128 * b, 128), 128)] = agg
        if k:
            agg_copy(k, b, rep).start()
        else:
            own_a[own_rows] = agg
    some_a = own_a.at[pl.ds(0, 448)]
    all_a = remote(some_a, some_a, as_.at[0], ar.at[0], in_rep(turn(rep, 1, REP)))
    pair_a = remote(lhs.at[mine_a], lhs.at[mine_a], ps.at[1], pr.at[1], pair)
    go(pair_a)
    finish()
    later[3].wait()
    later[4].wait()
    all_a.wait_recv()
    ends.append(all_a.wait_send)


    def g_copy(k, q, source):
        return remote(
            g_own.at[:, pl.ds(256 * (k % 2), 256)],
            g_all.at[pl.ds(pl.multiple_of(source * 128, 128), 128)],
            gs.at[0], gr.at[0], in_rep(q),
        )

    for half in range(2):
        cols = slice(256 * half, 256 * half + 256)
        pre = pre_self[:, cols] + dot(own_a[...], wn[:, cols], 0, 0)
        s = jax.nn.sigmoid(pre)
        g_own[:, cols] = (cot[:, cols].astype(F32) * (s * (1.0 + pre * (1.0 - s)))).astype(BF)
        out_ref[:, cols] = (pre * s).astype(BF)
        for step in (2, 1, 3):
            chip = turn(x, step, X)
            g_copy(2 * step + half, 2 * chip + half, rep).start()

        @pl.when(core != half)
        def _():
            g_copy(half, 2 * x + half, rep).start()

    some_g = g_all.at[pl.ds(0, 896)]
    all_g = remote(some_g, some_g, gs.at[0], gr.at[0], in_rep(turn(rep, 1, REP)))
    g_all[pl.ds(pl.multiple_of(rep * 128, 128), 128)] = g_own[
        :, pl.ds(pl.multiple_of(core * 256, 256), 256)
    ]
    finish()
    other = pl.ds(pl.multiple_of(64 - core * 64, 64), 64)
    other_a = pl.ds(pl.multiple_of(192 - core * 64, 64), 64)
    remote(lhs.at[other], lhs.at[other], ps.at[0], pr.at[0], pair).wait_recv()
    remote(lhs.at[other_a], lhs.at[other_a], ps.at[1], pr.at[1], pair).wait_recv()
    all_g.wait_recv()
    ends.append(all_g.wait_send)
    grad = dot(lhs[...], g_all[...], 1, 0)
    for q in range(4):
        cols = slice(64 * q, 64 * q + 64)
        part = jnp.concatenate([grad[:128, cols], grad[128:, cols]], axis=1)
        parts[q] = part.astype(BF)

    def part_copy(q, source):
        return remote(
            parts.at[q], y_in.at[source], ts.at[q], tr.at[source],
            {"rows": x * Z + z, "rep": 4 * core + q},
        )

    def part_stays(q):
        return jnp.logical_and(x == y, 4 * core + q == rep)

    for q in range(4):
        keep = pltpu.make_async_copy(parts.at[q], y_in.at[y], tr.at[y])
        stays = part_stays(q)
        pl.when(stays)(keep.start)
        pl.when(jnp.logical_not(stays))(part_copy(q, y).start)
    total = jnp.zeros((128, 128), F32)
    for source in range(4):
        part_copy(0, source).wait_recv()
        total = total + y_in[source].astype(F32)
    y_sum[...] = total.reshape(Z, 8, 128)

    def last_copy(j, source):
        a = turn(z, j, Z)
        return remote(
            y_sum.at[a], z_in.at[source], us.at[0], ur.at[0], in_rows(y, a)
        )

    for j in (8, 7, 9, 6, 10, 5, 11, 4, 12, 3, 13, 2, 14, 1, 15):
        last_copy(j, z).start()
    z_in[z] = y_sum[z]
    finish()
    for q in range(4):
        pl.when(jnp.logical_not(part_stays(q)))(part_copy(q, y).wait_send)
    some_z = z_in.at[pl.ds(0, Z - 1)]
    all_z = remote(some_z, some_z, us.at[0], ur.at[0], right)
    all_z.wait_recv()
    grads = z_in[0]
    for a in range(1, Z):
        grads = grads + z_in[a]
    wg_ref[0] = grads[:, :64]
    wg_ref[1] = grads[:, 64:]
    all_z.wait_send()


def local(features, neighbor_blocks, adjacency, w_self, w_neigh, cotangent):
    vmem, anywhere = pl.BlockSpec(memory_space=pltpu.VMEM), pl.BlockSpec(memory_space=pl.ANY)
    dma = pltpu.SemaphoreType.DMA
    return pl.pallas_call(
        kernel,
        out_shape=(
            jax.ShapeDtypeStruct((128, 512), BF),
            jax.ShapeDtypeStruct((2, 8, 64), F32),
        ),
        in_specs=[anywhere] * 6,
        out_specs=(vmem, vmem),
        scratch_shapes=[
            pltpu.VMEM((128, 64, 128), BF),
            pltpu.VMEM((8, 64, 128), BF),
            pltpu.VMEM((3, 16, 2, 64, 128), BF),
            pltpu.VMEM((3, 16, 2, 64, 128), BF),
            pltpu.VMEM((512, 128), BF),
            pltpu.VMEM((512, 128), BF),
            pltpu.VMEM((256, 1024), BF),
            pltpu.VMEM((8, 2, 128, 128), BF),
            pltpu.VMEM((512, 512), BF),
            pltpu.VMEM((512, 512), BF),
            pltpu.VMEM((128, 512), BF),
            pltpu.VMEM((8, 8, 128), F32),
            pltpu.VMEM((128, 512), F32),
            pltpu.VMEM((128, 512), BF),
            pltpu.VMEM((1024, 256), BF),
            pltpu.VMEM((4, 128, 128), BF),
            pltpu.VMEM((4, 128, 128), BF),
            pltpu.VMEM((16, 8, 128), F32),
            pltpu.VMEM((16, 8, 128), F32),
            pltpu.VMEM((64, 128), jnp.int32),
            pltpu.VMEM((3, 16, 128), jnp.int32),
            pltpu.VMEM((2, 8), jnp.int32),
            pltpu.SMEM((2, 8), jnp.int32),
            pltpu.SMEM((64, 128), jnp.int32),
            pltpu.SMEM((3, 16, 128), jnp.int32),
            dma((17,)),
            dma((2,)), dma((2, HALF, SUB)),
            dma((1,)), dma((1,)),
            dma((1,)), dma((1,)),
            dma((1,)), dma((1,)),
            dma((2,)), dma((2,)),
            dma((3,)), dma((3,)),
            dma((3,)), dma((3,)),
            dma((4,)), dma((4,)),
            dma((1,)), dma((1,)),
        ],
        compiler_params=pltpu.CompilerParams(
            collective_id=0, has_side_effects=True, vmem_limit_bytes=60 * 1024 * 1024
        ),
        cost_estimate=pl.CostEstimate(
            flops=500_000_000, bytes_accessed=2_500_000, transcendentals=65536
        ),
    )(neighbor_blocks.T, features.T, adjacency, w_self, w_neigh, cotangent)


def solution(mesh):
    in_specs = (
        P("rows", "rep"),
        P("rows", None),
        P("rows", None, None, None),
        P(),
        P(),
        P(("rows", "rep"), None),
    )
    out_specs = (P(("rows", "rep"), None), P(None, "rows", "rep"))
    return jax.shard_map(local, mesh=mesh, in_specs=in_specs, out_specs=out_specs, check_vma=False)
```

```python
import jax
import jax.numpy as jnp
from jax import lax
from jax.experimental import pallas as pl
from jax.experimental.pallas import tpu as pltpu
from jax.sharding import PartitionSpec as P

Y, Z, X = 4, 16, 4
REP = 2 * X
SUB = 4
PIECE = 8 // SUB
HALF = Z // 2
MESH = pl.DeviceIdType.MESH
BF, F32 = jnp.bfloat16, jnp.float32


def dot(a, b, ca, cb):
    return lax.dot_general(a, b, (((ca,), (cb,)), ((), ())), preferred_element_type=F32)


def kernel(
    nb_hbm, f_hbm, adj_hbm, ws_hbm, wn_hbm, cot_hbm,
    out_hbm, wg_ref,
    zbuf, hold, picked, used, own_f, own_a, lhs, adj, ws, wn, cot,
    scale, pre_self, g_own, g_all, parts, y_in, y_sum, z_in, table, asked, nb_v, nb_s, table_s, asked_s, out_v,
    load_sem, zs, zr, fs, fr, as_, ar, gs, gr, ps, pr, ns, nr, ys, yr, ts, tr, us, ur,
):
    row, rep = lax.axis_index("rows"), lax.axis_index("rep")
    y, z = row // Z, lax.rem(row, Z)
    x, core = rep // 2, lax.rem(rep, 2)

    def in_rows(yy, zz):
        return {"rows": yy * Z + zz, "rep": rep}

    def in_rep(q):
        return {"rows": row, "rep": q}

    def remote(src, dst, send, recv, device):
        return pltpu.make_async_remote_copy(
            src_ref=src, dst_ref=dst, send_sem=send, recv_sem=recv,
            device_id=device, device_id_type=MESH,
        )

    def turn(a, k, n):
        return lax.rem(a + k + n, n)

    right, left = in_rows(y, turn(z, 1, Z)), in_rows(y, turn(z, -1, Z))

    ends = []

    def go(copy):
        copy.start()
        ends.append(copy.wait_send)

    def finish():
        for end in ends:
            end()
        ends.clear()

    first = [
        pltpu.make_async_copy(
            f_hbm.at[:, pl.ds(128 * l, 128)], zbuf.at[z * 8 + l], load_sem.at[l]
        )
        for l in range(8)
    ]
    mine = pl.ds(pl.multiple_of(core * 64, 64), 64)
    mine_a = pl.ds(pl.multiple_of(128 + core * 64, 64), 64)
    later = [
        pltpu.make_async_copy(f_hbm, lhs.at[mine], load_sem.at[8]),
        pltpu.make_async_copy(adj_hbm, adj, load_sem.at[9]),
        pltpu.make_async_copy(ws_hbm, ws, load_sem.at[10]),
        pltpu.make_async_copy(wn_hbm, wn, load_sem.at[11]),
        pltpu.make_async_copy(cot_hbm, cot, load_sem.at[12]),
    ]
    numbers = pltpu.make_async_copy(nb_hbm, nb_v, load_sem.at[16])
    numbers.start()
    for c in first:
        c.start()

    barrier = pltpu.get_barrier_semaphore()
    for device in (right, left):
        pl.semaphore_signal(barrier, inc=1, device_id=device, device_id_type=MESH)
    for k in range(1, Y):
        pl.semaphore_signal(
            barrier, inc=1, device_id=in_rows(turn(y, k, Y), z), device_id_type=MESH
        )
    for k in range(1, REP):
        pl.semaphore_signal(
            barrier, inc=1, device_id=in_rep(turn(rep, k, REP)), device_id_type=MESH
        )
    for c in later:
        c.start()
    numbers.wait()
    owner_id = lax.broadcasted_iota(jnp.int32, (64, 8), 0)
    lane = lax.broadcasted_iota(jnp.int32, (64, 8), 1)
    low = jnp.full((64, 1), 255, jnp.int32)
    high = jnp.zeros((64, 1), jnp.int32)
    for k in range(2):
        block = nb_v[k : k + 1, :]
        named = block // 8 == owner_id
        code = (8 * k + lane) * 8 + block % 8
        low = jnp.minimum(low, jnp.min(jnp.where(named, code, 255), axis=1, keepdims=True))
        high = jnp.maximum(high, jnp.max(jnp.where(named, code, 0), axis=1, keepdims=True))
    lane = lax.broadcasted_iota(jnp.int32, (64, 128), 1)
    table[...] = jnp.where(lane == 0, low % 8, jnp.where(lane == 1, high % 8, low // 8))
    to_smem = [
        pltpu.make_async_copy(nb_v, nb_s, load_sem.at[13]),
        pltpu.make_async_copy(table, table_s, load_sem.at[14]),
    ]
    for c in to_smem:
        c.start()
    for c in first:
        c.wait()
    pl.semaphore_wait(barrier, 2 + (Y - 1) + (REP - 1))

    def table_copy(k):
        yy = turn(y, k, Y)
        return remote(
            table.at[pl.ds(yy * Z, Z)], asked.at[Y - k - 1], ns.at[k - 1], nr.at[k - 1],
            in_rows(yy, z),
        )


    def ring_copy(way, step, piece, chunk):
        at = pl.ds(chunk * 8 + piece * PIECE, PIECE)
        return remote(
            zbuf.at[at], zbuf.at[at], zs.at[way], zr.at[way, step, piece],
            right if way == 0 else left,
        )

    def sent(way, step, piece):
        return ring_copy(way, step, piece, turn(z, -step if way == 0 else step, Z))

    def arriving(way, step, piece):
        return ring_copy(way, step, piece, turn(z, -1 - step if way == 0 else 1 + step, Z))

    def last_way(piece):
        return 0 if piece < SUB // 2 else 1

    for way in range(2):
        sent(way, 0, 0).start()
    for k in (2, 1, 3):
        go(table_copy(k))
    for piece in range(1, SUB):
        for way in range(2):
            sent(way, 0, piece).start()

    def feature_copy(k, q, source):
        return remote(
            zbuf.at[z * 8 + q], own_f.at[pl.ds(pl.multiple_of(source * 64, 64), 64)],
            fs.at[0], fr.at[0], in_rep(q),
        )

    for k in range(1, REP):
        feature_copy(k, turn(rep, k, REP), rep).start()
    some_f = own_f.at[pl.ds(0, 448)]
    all_f = remote(some_f, some_f, fs.at[0], fr.at[0], in_rep(turn(rep, 1, REP)))
    ends.append(all_f.wait_send)
    later[0].wait()
    pair = in_rep(x * 2 + 1 - core)
    pair_f = remote(lhs.at[mine], lhs.at[mine], ps.at[0], pr.at[0], pair)
    go(pair_f)
    own_rows = pl.ds(pl.multiple_of(rep * 64, 64), 64)
    own_f[own_rows] = zbuf[z * 8 + rep]

    for k in range(1, Y):
        table_copy(k).wait_recv()
    ask_smem = pltpu.make_async_copy(asked, asked_s, load_sem.at[15])
    ask_smem.start()

    def use_copy(k, chunk):
        return remote(
            picked.at[k - 1, chunk], used.at[Y - k - 1, chunk],
            ys.at[k - 1], yr.at[Y - k - 1], in_rows(turn(y, k, Y), z),
        )

    def send_uses(chunk):
        hold[...] = zbuf[pl.ds(chunk * 8, 8)]
        for k in (2, 1, 3):
            for rank in range(2):
                picked[k - 1, chunk, rank] = hold[asked_s[k - 1, chunk, rank]]
            use_copy(k, chunk).start()

    def forward(step, pieces):
        for piece in pieces:
            for way in range(2):
                arriving(way, step - 1, piece).wait_recv()
                sent(way, step, piece).start()

    forward(1, range(SUB // 2))
    ask_smem.wait()
    send_uses(z)
    forward(1, range(SUB // 2, SUB))
    for way in range(2):
        send_uses(turn(z, -1 if way == 0 else 1, Z))

    def ring_step(step, carry):
        forward(step, range(SUB))
        for way in range(2):
            send_uses(turn(z, -step if way == 0 else step, Z))
        return carry

    lax.fori_loop(2, HALF - 1, ring_step, 0)
    for piece in range(SUB):
        for way in range(2):
            arriving(way, HALF - 2, piece).wait_recv()
            if way == last_way(piece):
                sent(way, HALF - 1, piece).start()
    for way in range(2):
        send_uses(turn(z, 1 - HALF if way == 0 else HALF - 1, Z))
    for piece in range(SUB):
        arriving(last_way(piece), HALF - 1, piece).wait_recv()
    send_uses(turn(z, HALF, Z))

    def ring_end():
        for way in range(2):
            all_sent = zbuf.at[pl.ds(0, 8 * HALF - 4)]
            remote(all_sent, all_sent, zs.at[way], zr.at[way, 0, 0], right).wait_send()

    ends.append(ring_end)

    def all_uses(k):
        return remote(
            picked.at[k - 1], used.at[Y - k - 1], ys.at[k - 1], yr.at[Y - k - 1],
            in_rows(turn(y, k, Y), z),
        )

    def uses_left():
        for k in range(1, Y):
            all_uses(k).wait_send()

    ends.append(uses_left)
    later[1].wait()
    ones = jnp.ones((8, 128), BF)
    for b in range(8):
        total = dot(ones, adj[b, 0], 1, 1) + dot(ones, adj[b, 1], 1, 1)
        scale[b] = 1.0 / jnp.sqrt(1.0 + total)
    for c in to_smem:
        c.wait()
    all_f.wait_recv()
    later[2].wait()
    pre_self[...] = dot(own_f[...], ws[...], 0, 0)
    for k in range(1, Y):
        all_uses(k).wait_recv()
    def use(k, b):
        block = nb_s[k, b]
        owner = block // 8
        ahead = lax.rem(owner // Z - y + Y, Y)
        rank = jnp.where(table_s[owner, 2] == 8 * k + b, 0, 1)
        other = used[jnp.maximum(ahead, 1) - 1, lax.rem(owner, Z), rank]
        return jnp.where(ahead == 0, zbuf[lax.rem(block, 8 * Z)], other)

    def agg_copy(k, q, source):
        return remote(
            lhs.at[mine_a, pl.ds(pl.multiple_of(q * 128, 128), 128)],
            own_a.at[pl.ds(pl.multiple_of(source * 64, 64), 64)],
            as_.at[0], ar.at[0], in_rep(q),
        )

    for k in (4, 3, 5, 2, 6, 1, 7, 0):
        b = turn(rep, k, REP)
        raw = dot(use(0, b), adj[b, 0], 1, 1) + dot(use(1, b), adj[b, 1], 1, 1)
        agg = (raw * scale[b, 0:1, :]).astype(BF)
        lhs[mine_a, pl.ds(pl.multiple_of(128 * b, 128), 128)] = agg
        if k:
            agg_copy(k, b, rep).start()
        else:
            own_a[own_rows] = agg
    some_a = own_a.at[pl.ds(0, 448)]
    all_a = remote(some_a, some_a, as_.at[0], ar.at[0], in_rep(turn(rep, 1, REP)))
    pair_a = remote(lhs.at[mine_a], lhs.at[mine_a], ps.at[1], pr.at[1], pair)
    go(pair_a)
    finish()
    later[3].wait()
    later[4].wait()
    all_a.wait_recv()
    ends.append(all_a.wait_send)


    def g_copy(k, q, source):
        return remote(
            g_own.at[:, pl.ds(256 * (k % 2), 256)],
            g_all.at[pl.ds(pl.multiple_of(source * 128, 128), 128)],
            gs.at[0], gr.at[0], in_rep(q),
        )

    for half in range(2):
        cols = slice(256 * half, 256 * half + 256)
        pre = pre_self[:, cols] + dot(own_a[...], wn[:, cols], 0, 0)
        s = jax.nn.sigmoid(pre)
        g_own[:, cols] = (cot[:, cols].astype(F32) * (s * (1.0 + pre * (1.0 - s)))).astype(BF)
        out_v[:, cols] = (pre * s).astype(BF)
        for step in (2, 1, 3):
            chip = turn(x, step, X)
            g_copy(2 * step + half, 2 * chip + half, rep).start()

        @pl.when(core != half)
        def _():
            g_copy(half, 2 * x + half, rep).start()

    write = pltpu.make_async_copy(out_v, out_hbm, load_sem.at[17])
    write.start()
    some_g = g_all.at[pl.ds(0, 896)]
    all_g = remote(some_g, some_g, gs.at[0], gr.at[0], in_rep(turn(rep, 1, REP)))
    g_all[pl.ds(pl.multiple_of(rep * 128, 128), 128)] = g_own[
        :, pl.ds(pl.multiple_of(core * 256, 256), 256)
    ]
    finish()
    other = pl.ds(pl.multiple_of(64 - core * 64, 64), 64)
    other_a = pl.ds(pl.multiple_of(192 - core * 64, 64), 64)
    remote(lhs.at[other], lhs.at[other], ps.at[0], pr.at[0], pair).wait_recv()
    remote(lhs.at[other_a], lhs.at[other_a], ps.at[1], pr.at[1], pair).wait_recv()
    all_g.wait_recv()
    ends.append(all_g.wait_send)
    grad = dot(lhs[...], g_all[...], 1, 0)
    for q in range(4):
        cols = slice(64 * q, 64 * q + 64)
        part = jnp.concatenate([grad[:128, cols], grad[128:, cols]], axis=1)
        parts[q] = part.astype(BF)

    def part_copy(q, source):
        return remote(
            parts.at[q], y_in.at[source], ts.at[q], tr.at[source],
            {"rows": x * Z + z, "rep": 4 * core + q},
        )

    def part_stays(q):
        return jnp.logical_and(x == y, 4 * core + q == rep)

    for q in range(4):
        keep = pltpu.make_async_copy(parts.at[q], y_in.at[y], tr.at[y])
        stays = part_stays(q)
        pl.when(stays)(keep.start)
        pl.when(jnp.logical_not(stays))(part_copy(q, y).start)
    total = jnp.zeros((128, 128), F32)
    for source in range(4):
        part_copy(0, source).wait_recv()
        total = total + y_in[source].astype(F32)
    y_sum[...] = total.reshape(Z, 8, 128)

    def last_copy(j, source):
        a = turn(z, j, Z)
        return remote(
            y_sum.at[a], z_in.at[source], us.at[0], ur.at[0], in_rows(y, a)
        )

    for j in (8, 7, 9, 6, 10, 5, 11, 4, 12, 3, 13, 2, 14, 1, 15):
        last_copy(j, z).start()
    z_in[z] = y_sum[z]
    finish()
    for q in range(4):
        pl.when(jnp.logical_not(part_stays(q)))(part_copy(q, y).wait_send)
    some_z = z_in.at[pl.ds(0, Z - 1)]
    all_z = remote(some_z, some_z, us.at[0], ur.at[0], right)
    all_z.wait_recv()
    grads = z_in[0]
    for a in range(1, Z):
        grads = grads + z_in[a]
    wg_ref[0] = grads[:, :64]
    wg_ref[1] = grads[:, 64:]
    all_z.wait_send()
    write.wait()


def local(features, neighbor_blocks, adjacency, w_self, w_neigh, cotangent):
    vmem, anywhere = pl.BlockSpec(memory_space=pltpu.VMEM), pl.BlockSpec(memory_space=pl.ANY)
    dma = pltpu.SemaphoreType.DMA
    return pl.pallas_call(
        kernel,
        out_shape=(
            jax.ShapeDtypeStruct((128, 512), BF),
            jax.ShapeDtypeStruct((2, 8, 64), F32),
        ),
        in_specs=[anywhere] * 6,
        out_specs=(anywhere, vmem),
        scratch_shapes=[
            pltpu.VMEM((128, 64, 128), BF),
            pltpu.VMEM((8, 64, 128), BF),
            pltpu.VMEM((3, 16, 2, 64, 128), BF),
            pltpu.VMEM((3, 16, 2, 64, 128), BF),
            pltpu.VMEM((512, 128), BF),
            pltpu.VMEM((512, 128), BF),
            pltpu.VMEM((256, 1024), BF),
            pltpu.VMEM((8, 2, 128, 128), BF),
            pltpu.VMEM((512, 512), BF),
            pltpu.VMEM((512, 512), BF),
            pltpu.VMEM((128, 512), BF),
            pltpu.VMEM((8, 8, 128), F32),
            pltpu.VMEM((128, 512), F32),
            pltpu.VMEM((128, 512), BF),
            pltpu.VMEM((1024, 256), BF),
            pltpu.VMEM((4, 128, 128), BF),
            pltpu.VMEM((4, 128, 128), BF),
            pltpu.VMEM((16, 8, 128), F32),
            pltpu.VMEM((16, 8, 128), F32),
            pltpu.VMEM((64, 128), jnp.int32),
            pltpu.VMEM((3, 16, 128), jnp.int32),
            pltpu.VMEM((2, 8), jnp.int32),
            pltpu.SMEM((2, 8), jnp.int32),
            pltpu.SMEM((64, 128), jnp.int32),
            pltpu.SMEM((3, 16, 128), jnp.int32),
            pltpu.VMEM((128, 512), BF),
            dma((18,)),
            dma((2,)), dma((2, HALF, SUB)),
            dma((1,)), dma((1,)),
            dma((1,)), dma((1,)),
            dma((1,)), dma((1,)),
            dma((2,)), dma((2,)),
            dma((3,)), dma((3,)),
            dma((3,)), dma((3,)),
            dma((4,)), dma((4,)),
            dma((1,)), dma((1,)),
        ],
        compiler_params=pltpu.CompilerParams(
            collective_id=0, has_side_effects=True, vmem_limit_bytes=60 * 1024 * 1024
        ),
        cost_estimate=pl.CostEstimate(
            flops=500_000_000, bytes_accessed=2_500_000, transcendentals=65536
        ),
    )(neighbor_blocks.T, features.T, adjacency, w_self, w_neigh, cotangent)


def solution(mesh):
    in_specs = (
        P("rows", "rep"),
        P("rows", None),
        P("rows", None, None, None),
        P(),
        P(),
        P(("rows", "rep"), None),
    )
    out_specs = (P(("rows", "rep"), None), P(None, "rows", "rep"))
    return jax.shard_map(local, mesh=mesh, in_specs=in_specs, out_specs=out_specs, check_vma=False)
```
